256 devices in a mesh: tm: 4 (over z_lo, core), space: 64 (over y, z_hi, x).
Axes of the slice: x: 4, y: 4, z: 8 (z_hi: 4, z_lo: 2; z = z_hi * 2 + z_lo), core: 2. Of those that a mesh axis runs over, the one named last changes fastest.
Arguments:
- starts: float32 [4, 2, 256, 128, 128], P('tm', None, 'space'), may hold values from 0 to 1
- feed_rate: float32 [256, 128, 128], P('space'), may hold values from 0.02 to 0.2
- kill_rate: float32 [256, 128, 128], P('space'), may hold values from 0.04 to 0.2
Outputs:
- slice_ends: float32 [4, 2, 256, 128, 128], P('tm', None, 'space')
The draws below stay inside these ranges and needn't reach their ends.
All inputs are finite; a program needn't handle non-finite values.
Results may differ from the reference program's by a relative error of at most 0.00002.
Values sent between devices are 32-bit elements; how exact they have to be, the bound alone decides.
No kernel may reach another device: no remote copies, remote signals or barrier semaphores. Data moves between devices by JAX's collectives and lax.ppermute only.
A program may use at most 64 MiB of HBM per device.

```python
import math
import jax
import jax.numpy as jnp

NY = 128
NZ = 128
SUBSTEPS = 4
SWEEPS = 4
SLICES = 4
NX = 256


def block_levels(rng, dims, pieces, smallest, high):
    def one(position, shards_of):
        steps = jax.random.uniform(jax.random.fold_in(jax.random.fold_in(rng, 6), position), (shards_of,), jnp.float32, smallest / len(pieces), high / len(pieces))
        return jnp.repeat(jnp.exp(steps), dims[position] // shards_of).reshape((-1,) + (1,) * (len(dims) - position - 1))

    loudness = one(*pieces[0])
    for cut in pieces[1:]:
        loudness = loudness * one(*cut)
    return loudness


def setup_inputs(seed: int = 0) -> dict:
    arg_keys = jax.random.split(jax.random.key(seed), 4)
    return {
        "starts": jnp.clip(1.0 * jax.random.uniform(arg_keys[0], (SLICES, 2, NX, NY, NZ), jnp.float32) ** block_levels(arg_keys[0], (SLICES, 2, NX, NY, NZ), ((0, 4), (2, 64)), -0.2, 0.2), 0.0, 1.0),
        "feed_rate": jnp.clip(jnp.exp(math.log(0.2) - 2.3025851 * jax.random.uniform(arg_keys[1], (NX, NY, NZ), jnp.float32) ** block_levels(arg_keys[1], (NX, NY, NZ), ((0, 64),), -0.2, 0.2)), 0.02, 0.2),
        "kill_rate": jnp.clip(jnp.exp(math.log(0.2) - 1.609438 * jax.random.uniform(arg_keys[2], (NX, NY, NZ), jnp.float32) ** block_levels(arg_keys[2], (NX, NY, NZ), ((0, 64),), -0.2, 0.2)), 0.04, 0.2),
    }


SIDE_WEIGHT = 2.0 ** (-2.0 / 3.0)
MIDDLE_WEIGHT = 2.0 ** (1.0 / 3.0)
FINE_RATES = (0.4, 0.2)
TIME_STEP = 0.25


def diffusion():
    return jnp.array(FINE_RATES, jnp.float32).reshape(2, 1, 1, 1)


def shifted(fields, axis):
    return jnp.roll(fields, 1, axis), jnp.roll(fields, -1, axis)


def smooth_line(backward, centre, forward):
    return SIDE_WEIGHT * (backward + forward) + MIDDLE_WEIGHT * centre


def stencil_full(fields):
    backward, forward = shifted(fields, 1)
    along_x = smooth_line(backward, fields, forward)
    backward, forward = shifted(along_x, 2)
    along_y = smooth_line(backward, along_x, forward)
    backward, forward = shifted(along_y, 3)
    along_z = smooth_line(backward, along_y, forward)
    return 0.25 * (along_z - 16.0 * fields)


def reaction(fields, coefficients):
    substrate = fields[0]
    catalyst = fields[1]
    encounter = substrate * catalyst * catalyst
    first_term = -encounter + coefficients[0] * (1.0 - substrate)
    second_term = encounter - (coefficients[0] + coefficients[1]) * catalyst
    return jnp.stack([first_term, second_term])


def fine_full(fields, coefficients):
    current = fields
    for substep in range(SUBSTEPS):
        current = current + diffusion() * stencil_full(current) + TIME_STEP * reaction(current, coefficients)
    return current


def coarse_full(fields, coefficients):
    coarse_span = float(SUBSTEPS)
    implicit = coarse_span * diffusion()
    explicit_side = fields + (coarse_span * TIME_STEP) * reaction(fields, coefficients)
    iterate = explicit_side
    for sweep_index in range(SWEEPS):
        backward, forward = shifted(iterate, 1)
        neighbours = backward + forward
        backward, forward = shifted(iterate, 2)
        neighbours = neighbours + backward + forward
        backward, forward = shifted(iterate, 3)
        neighbours = neighbours + backward + forward
        iterate = (explicit_side + implicit * neighbours) / (1.0 + 6.0 * implicit)
    return iterate


def reference(starts, feed_rate, kill_rate):
    coefficients = jnp.stack([feed_rate, kill_rate])
    corrections = []
    for slice_index in range(SLICES):
        fine_end = fine_full(starts[slice_index], coefficients)
        corrections.append(fine_end - coarse_full(starts[slice_index], coefficients))
    handed = starts[0]
    results = []
    for slice_index in range(SLICES):
        handed = coarse_full(handed, coefficients) + corrections[slice_index]
        results.append(handed)
    return jnp.stack(results)
```

```python
import jax
import jax.numpy as jnp
from jax import lax
from jax.experimental import pallas as pl
from jax.experimental.pallas import tpu as pltpu
from jax.sharding import PartitionSpec as P

SUBSTEPS = 4
SWEEPS = 4
FINE_RATES = (0.4, 0.2)
TIME_STEP = 0.25
COARSE_STEP = SUBSTEPS * TIME_STEP
VMEM = pl.BlockSpec(memory_space=pltpu.VMEM)
SMEM = pl.BlockSpec(memory_space=pltpu.SMEM)
AXES = ("tm", "space")


def triple(values, axis):
    pairs = values + pltpu.roll(values, 1, axis)
    return pairs + pltpu.roll(pairs, values.shape[axis] - 1, axis)


def around(values):
    lines = pltpu.roll(values, 1, 0) + pltpu.roll(values, values.shape[0] - 1, 0)
    rows = pltpu.roll(values, 1, 1) + pltpu.roll(values, values.shape[1] - 1, 1)
    return lines + rows


def rates_of(substrate, catalyst, feed, kill):
    encounter = substrate * catalyst * catalyst
    return feed * (1.0 - substrate) - encounter, encounter - (feed + kill) * catalyst


def fine_layer(below, centre, above, feed, kill):
    reactions = rates_of(centre[0], centre[1], feed, kill)
    fields = []
    for species, rate in enumerate(FINE_RATES):
        sums = (below[species] + above[species]) + 2.0 * centre[species]
        sums = triple(triple(sums, 0), 1)
        fields.append(
            (1.0 - 4.0 * rate) * centre[species]
            + (rate / 16.0) * sums
            + TIME_STEP * reactions[species]
        )
    return fields


def sweep_layer(species, below, centre, above, explicit):
    implicit = SUBSTEPS * FINE_RATES[species]
    scale = 1.0 / (1.0 + 6.0 * implicit)
    return scale * explicit + (implicit * scale) * ((below + above) + around(centre))


def explicit_layer(substrate, catalyst, feed, kill):
    first, second = rates_of(substrate, catalyst, feed, kill)
    return substrate + COARSE_STEP * first, catalyst + COARSE_STEP * second


def joined(low, own, high, depth):
    def read(species, layer):
        part = (low, own, high)[layer // depth]
        return part[species, layer % depth]

    return read


def fine_levels(read, coefficient, levels, out, depth):
    count = 3 * depth - 2
    first = levels[0]
    for layer in range(count):
        fields = [[read(species, layer + shift) for species in (0, 1)] for shift in (0, 1, 2)]
        new = fine_layer(*fields, coefficient(0, layer + 1), coefficient(1, layer + 1))
        first[0, layer] = new[0]
        first[1, layer] = new[1]
    source = first
    for substep in range(1, SUBSTEPS):
        count -= 2
        target = out if substep == SUBSTEPS - 1 else levels[substep % 2]
        for layer in range(count):
            place = layer + substep + 1
            fields = [[source[species, layer + shift] for species in (0, 1)] for shift in (0, 1, 2)]
            new = fine_layer(*fields, coefficient(0, place), coefficient(1, place))
            target[0, layer] = new[0]
            target[1, layer] = new[1]
        source = target


def coarse_levels(read, levels, finish, depth):
    count = 3 * depth - 2
    for layer in range(count):
        for species in (0, 1):
            centre = read(species, layer + 1)
            levels[0][species, layer] = sweep_layer(
                species, read(species, layer), centre, read(species, layer + 2), centre
            )
    for sweep in range(1, SWEEPS):
        count -= 2
        source, target = levels[(sweep - 1) % 2], levels[sweep % 2]
        for layer in range(count):
            new = [
                sweep_layer(
                    species,
                    source[species, layer],
                    source[species, layer + 1],
                    source[species, layer + 2],
                    read(species, layer + sweep + 1),
                )
                for species in (0, 1)
            ]
            if sweep == SWEEPS - 1:
                finish(layer, new)
            else:
                target[0, layer] = new[0]
                target[1, layer] = new[1]


def fine_kernel(flag, low, own, high, low_c, feed, kill, high_c, state, explicit, level_a, level_b):
    depth = own.shape[1]

    @pl.when(flag[0] == 1)
    def _():
        def coefficient(which, layer):
            if layer < depth:
                return low_c[2 + which, layer]
            if layer >= 2 * depth:
                return high_c[2 + which, layer - 2 * depth]
            return (feed, kill)[which][layer - depth]

        fine_levels(joined(low, own, high, depth), coefficient, (level_a, level_b), state, depth)
        for layer in range(depth):
            new = explicit_layer(state[0, layer], state[1, layer], feed[layer], kill[layer])
            explicit[0, layer] = new[0]
            explicit[1, layer] = new[1]


def correction_kernel(flag, low, own, feed, kill, high, correction, level_a, level_b, wide):
    depth = own.shape[1]

    @pl.when(flag[0] == 1)
    def _():
        def coefficient(which, layer):
            if layer < depth:
                return low[2 + which, layer]
            if layer >= 2 * depth:
                return high[2 + which, layer - 2 * depth]
            return (feed, kill)[which][layer - depth]

        read = joined(low, own, high, depth)
        fine_levels(read, coefficient, (level_a, level_b), correction, depth)
        for layer in range(3 * depth):
            new = explicit_layer(
                read(0, layer), read(1, layer), coefficient(0, layer), coefficient(1, layer)
            )
            wide[0, layer] = new[0]
            wide[1, layer] = new[1]

        def finish(layer, new):
            for species in (0, 1):
                correction[species, layer] = correction[species, layer] - new[species]

        coarse_levels(lambda species, layer: wide[species, layer], (level_a, level_b), finish, depth)


def coarse_kernel(flag, low, own, high, correction, feed, kill, state, explicit, level_a, level_b):
    depth = own.shape[1]

    @pl.when(flag[0] == 1)
    def _():
        def finish(layer, new):
            first = new[0] + correction[0, layer]
            second = new[1] + correction[1, layer]
            state[0, layer] = first
            state[1, layer] = second
            explicit[0, layer], explicit[1, layer] = explicit_layer(
                first, second, feed[layer], kill[layer]
            )

        coarse_levels(joined(low, own, high, depth), (level_a, level_b), finish, depth)


def run(body, flag, operands, outputs, wide=False):
    shape = operands[1].shape
    depth, plane = shape[1], shape[2:]
    slab = jax.ShapeDtypeStruct((2, depth, *plane), jnp.float32)
    scratch = [
        pltpu.VMEM((2, 3 * depth - 2, *plane), jnp.float32),
        pltpu.VMEM((2, 3 * depth - 4, *plane), jnp.float32),
    ]
    if wide:
        scratch.append(pltpu.VMEM((2, 3 * depth, *plane), jnp.float32))
    return pl.pallas_call(
        body,
        out_shape=[slab] * outputs,
        in_specs=[SMEM] + [VMEM] * len(operands),
        out_specs=[VMEM] * outputs,
        scratch_shapes=scratch,
        compiler_params=pltpu.CompilerParams(vmem_limit_bytes=24 * 2**20),
        cost_estimate=pl.CostEstimate(flops=10**7, bytes_accessed=2**21, transcendentals=0),
    )(flag.astype(jnp.int32).reshape(1), *operands)


def shards(starts, feed, kill):
    own = starts[0]
    slabs = lax.axis_size("space")
    slices = lax.axis_size("tm")
    position = lax.axis_index("tm")

    def moved(array, routes, shift=0):
        pairs = []
        for source, target in routes:
            for slab in range(slabs):
                pairs.append((source * slabs + slab, target * slabs + (slab + shift) % slabs))
        return lax.ppermute(array, AXES, pairs)

    def spread(array, source, target):
        low = moved(array, [(source, target)], 1)
        high = moved(array, [(source, target)], -1)
        return low, moved(array, [(source, target)]), high

    everyone = [(index, index) for index in range(slices)]
    crossed = moved(own, [(0, 3)])
    package = jnp.concatenate([own, feed[None], kill[None]])
    low = moved(package, everyone, 1)
    high = moved(package, everyone, -1)
    first = spread(crossed, 3, 2)
    state, explicit = run(
        fine_kernel, position == 2, (*first, low, feed, kill, high), 2
    )
    second = spread(explicit, 2, 3)
    (correction,) = run(
        correction_kernel, position >= 1, (low, own, feed, kill, high), 1, wide=True
    )
    lent = moved(correction, [(1, 3)])
    state_b, explicit = run(
        coarse_kernel, position == 3, (*second, lent, feed, kill), 2
    )
    third = spread(explicit, 3, 2)
    back = moved(jnp.where(position == 2, state, state_b), [(2, 0), (3, 1)])
    state_c, explicit = run(
        coarse_kernel, position == 2, (*third, correction, feed, kill), 2
    )
    fourth = spread(explicit, 2, 3)
    state_d, _ = run(
        coarse_kernel, position == 3, (*fourth, correction, feed, kill), 2
    )
    result = jnp.where(position < 2, back, jnp.where(position == 2, state_c, state_d))
    return result[None]


def solution(mesh):
    placed = (P("tm", None, "space", None, None), P("space", None, None), P("space", None, None))
    return jax.shard_map(
        shards,
        mesh=mesh,
        in_specs=placed,
        out_specs=P("tm", None, "space", None, None),
        check_vma=False,
    )
```

```python
import jax
import jax.numpy as jnp
from jax import lax
from jax.experimental import pallas as pl
from jax.experimental.pallas import tpu as pltpu
from jax.sharding import PartitionSpec as P

SUBSTEPS = 4
SWEEPS = 4
FINE_RATES = (0.4, 0.2)
TIME_STEP = 0.25
COARSE_STEP = SUBSTEPS * TIME_STEP
VMEM = pl.BlockSpec(memory_space=pltpu.VMEM)
SMEM = pl.BlockSpec(memory_space=pltpu.SMEM)
ANY = pl.BlockSpec(memory_space=pl.ANY)
AXES = ("tm", "space")


def triple(values, axis):
    pairs = values + pltpu.roll(values, 1, axis)
    return pairs + pltpu.roll(pairs, values.shape[axis] - 1, axis)


def around(values):
    lines = pltpu.roll(values, 1, 0) + pltpu.roll(values, values.shape[0] - 1, 0)
    rows = pltpu.roll(values, 1, 1) + pltpu.roll(values, values.shape[1] - 1, 1)
    return lines + rows


def rates_of(substrate, catalyst, feed, kill):
    encounter = substrate * catalyst * catalyst
    return feed * (1.0 - substrate) - encounter, encounter - (feed + kill) * catalyst


def fine_layer(below, centre, above, feed, kill):
    reactions = rates_of(centre[0], centre[1], feed, kill)
    fields = []
    for species, rate in enumerate(FINE_RATES):
        sums = (below[species] + above[species]) + 2.0 * centre[species]
        sums = triple(triple(sums, 0), 1)
        fields.append(
            (1.0 - 4.0 * rate) * centre[species]
            + (rate / 16.0) * sums
            + TIME_STEP * reactions[species]
        )
    return fields


def sweep_layer(species, below, centre, above, explicit):
    implicit = SUBSTEPS * FINE_RATES[species]
    scale = 1.0 / (1.0 + 6.0 * implicit)
    return scale * explicit + (implicit * scale) * ((below + above) + around(centre))


def explicit_layer(substrate, catalyst, feed, kill):
    first, second = rates_of(substrate, catalyst, feed, kill)
    return substrate + COARSE_STEP * first, catalyst + COARSE_STEP * second


def joined(low, own, high, depth):
    def read(species, layer):
        part = (low, own, high)[layer // depth]
        return part[species, layer % depth]

    return read


def fine_levels(read, coefficient, levels, out, depth):
    count = 3 * depth - 2
    first = levels[0]
    for layer in range(count):
        fields = [[read(species, layer + shift) for species in (0, 1)] for shift in (0, 1, 2)]
        new = fine_layer(*fields, coefficient(0, layer + 1), coefficient(1, layer + 1))
        first[0, layer] = new[0]
        first[1, layer] = new[1]
    source = first
    for substep in range(1, SUBSTEPS):
        count -= 2
        target = out if substep == SUBSTEPS - 1 else levels[substep % 2]
        for layer in range(count):
            place = layer + substep + 1
            fields = [[source[species, layer + shift] for species in (0, 1)] for shift in (0, 1, 2)]
            new = fine_layer(*fields, coefficient(0, place), coefficient(1, place))
            target[0, layer] = new[0]
            target[1, layer] = new[1]
        source = target


def coarse_levels(read, levels, finish, depth):
    count = 3 * depth - 2
    for layer in range(count):
        for species in (0, 1):
            centre = read(species, layer + 1)
            levels[0][species, layer] = sweep_layer(
                species, read(species, layer), centre, read(species, layer + 2), centre
            )
    for sweep in range(1, SWEEPS):
        count -= 2
        source, target = levels[(sweep - 1) % 2], levels[sweep % 2]
        for layer in range(count):
            new = [
                sweep_layer(
                    species,
                    source[species, layer],
                    source[species, layer + 1],
                    source[species, layer + 2],
                    read(species, layer + sweep + 1),
                )
                for species in (0, 1)
            ]
            if sweep == SWEEPS - 1:
                finish(layer, new)
            else:
                target[0, layer] = new[0]
                target[1, layer] = new[1]


def coefficients_of(low, feed, kill, high, depth):
    def coefficient(which, layer):
        if layer < depth:
            return low[which, layer]
        if layer >= 2 * depth:
            return high[which, layer - 2 * depth]
        return (feed, kill)[which][layer - depth]

    return coefficient


def fine_kernel(worker, position, low, own, high, low_c, feed, kill, high_c, state, explicit, *levels):
    depth = own.shape[1]

    @pl.when((position[0] == worker[0]) | (position[0] == worker[-1]))
    def _():
        coefficient = coefficients_of(low_c, feed, kill, high_c, depth)
        fine_levels(joined(low, own, high, depth), coefficient, levels, state, depth)
        for layer in range(depth):
            new = explicit_layer(state[0, layer], state[1, layer], feed[layer], kill[layer])
            explicit[0, layer] = new[0]
            explicit[1, layer] = new[1]


def correction_kernel(
    worker, position, low, own, high, low_c, feed, kill, high_c, correction, level_a, level_b, wide
):
    depth = own.shape[1]

    @pl.when((position[0] == worker[0]) | (position[0] == worker[-1]))
    def _():
        coefficient = coefficients_of(low_c, feed, kill, high_c, depth)
        read = joined(low, own, high, depth)
        fine_levels(read, coefficient, (level_a, level_b), correction, depth)
        for layer in range(3 * depth):
            new = explicit_layer(
                read(0, layer), read(1, layer), coefficient(0, layer), coefficient(1, layer)
            )
            wide[0, layer] = new[0]
            wide[1, layer] = new[1]

        def finish(layer, new):
            for species in (0, 1):
                correction[species, layer] = correction[species, layer] - new[species]

        coarse_levels(lambda species, layer: wide[species, layer], (level_a, level_b), finish, depth)


def coarse_kernel(worker, position, low, own, high, correction, feed, kill, state, explicit, *levels):
    depth = own.shape[1]

    @pl.when((position[0] == worker[0]) | (position[0] == worker[-1]))
    def _():
        def finish(layer, new):
            first = new[0] + correction[0, layer]
            second = new[1] + correction[1, layer]
            state[0, layer] = first
            state[1, layer] = second
            explicit[0, layer], explicit[1, layer] = explicit_layer(
                first, second, feed[layer], kill[layer]
            )

        coarse_levels(joined(low, own, high, depth), levels, finish, depth)


def last_kernel(worker, position, low, own, high, correction, third, back, state, *levels):
    depth = own.shape[1]

    @pl.when(position[0] < worker[0] - 1)
    def _():
        state[...] = back[...]

    @pl.when(position[0] == worker[0] - 1)
    def _():
        state[...] = third[...]

    @pl.when((position[0] == worker[0]) | (position[0] == worker[-1]))
    def _():
        def finish(layer, new):
            for species in (0, 1):
                state[species, layer] = new[species] + correction[species, layer]

        coarse_levels(joined(low, own, high, depth), levels, finish, depth)


def stack_kernel(position, feed, kill, both):
    both[0] = feed[...]
    both[1] = kill[...]


def run(body, position, operands, outputs, scratch=2, pinned=True, worker=None, tokens=()):
    depth, plane = operands[0].shape[-3], operands[0].shape[-2:]
    shape = (2, depth, *plane)
    if pinned:
        out_shape = [pltpu.VMEM(shape, jnp.float32)] * outputs
    else:
        out_shape = [jax.ShapeDtypeStruct(shape, jnp.float32)] * outputs
    layers = (3 * depth - 2, 3 * depth - 4, 3 * depth)[:scratch]
    operands = [pltpu.with_memory_space_constraint(array, pltpu.VMEM) for array in operands]

    count = 1 + len(operands)

    def kernel(*refs):
        refs = refs[:count] + refs[count + len(tokens) :]
        body(*(() if worker is None else (worker,)), *refs)

    return pl.pallas_call(
        kernel,
        out_shape=out_shape,
        in_specs=[SMEM] + [VMEM] * len(operands) + [ANY] * len(tokens),
        out_specs=[VMEM] * outputs,
        scratch_shapes=[pltpu.VMEM((2, count, *plane), jnp.float32) for count in layers],
        compiler_params=pltpu.CompilerParams(vmem_limit_bytes=12 * 2**20),
        cost_estimate=pl.CostEstimate(flops=10**10, bytes_accessed=2**21, transcendentals=0),
    )(position, *operands, *tokens)


def copy_kernel(array, token, copied):
    copied[...] = array[...]


def after(array, token):
    return pl.pallas_call(
        copy_kernel,
        out_shape=pltpu.VMEM(array.shape, array.dtype),
        in_specs=[VMEM, ANY],
        out_specs=VMEM,
        compiler_params=pltpu.CompilerParams(vmem_limit_bytes=4 * 2**20),
    )(array, token)


def shards(starts, feed, kill):
    own = starts[0]
    slabs = lax.axis_size("space")
    position = lax.axis_index("tm").astype(jnp.int32).reshape(1)

    def moved(array, routes, shift=0):
        pairs = []
        for source, target in routes:
            for slab in range(slabs):
                pairs.append((source * slabs + slab, target * slabs + (slab + shift) % slabs))
        return lax.ppermute(array, AXES, pairs)

    def sides(array, routes):
        return moved(array, routes, 1), moved(array, routes, -1)

    def spread(array, source, target):
        low, high = sides(array, [(source, target)])
        return low, moved(array, [(source, target)]), high

    crossed = moved(own, [(0, 3)])
    lent = moved(own, [(1, 0)])
    (both,) = run(stack_kernel, position, (feed, kill), 1, 0)
    low_c, high_c = sides(both, [(2, 2)])
    first = spread(crossed, 3, 2)
    lent = moved(after(lent, crossed), [(0, 3)])
    low_d = moved(after(low_c, first[1]), [(2, 3)])
    high_d = moved(after(high_c, first[1]), [(2, 3)])
    low_1, high_1 = sides(lent, [(3, 3)])
    ends, explicit = run(
        fine_kernel,
        position,
        (*first, low_c, feed, kill, high_c),
        2,
        worker=(2,),
        tokens=(low_d, high_d, lent),
    )
    second = spread(explicit, 2, 3)
    (correction,) = run(
        correction_kernel,
        position,
        (low_1, lent, high_1, low_d, feed, kill, high_d),
        1,
        3,
        worker=(3,),
    )
    own_2 = after(own, second[1])
    low_2, high_2 = sides(own_2, [(2, 2)])
    ends_b, explicit = run(
        coarse_kernel,
        position,
        (*second, correction, feed, kill),
        2,
        worker=(3,),
        tokens=(own_2,),
    )
    third = spread(explicit, 3, 2)
    back = moved(jnp.where(position[0] == 2, ends, ends_b), [(2, 0), (3, 1)])
    own_3 = after(own, third[1])
    low_3, high_3 = sides(own_3, [(3, 3)])
    (correction,) = run(
        correction_kernel,
        position,
        (low_2, own_2, high_2, low_c, feed, kill, high_c),
        1,
        3,
        worker=(2,),
    )
    ends_c, explicit = run(
        coarse_kernel, position, (*third, correction, feed, kill), 2, worker=(2,)
    )
    fourth = spread(explicit, 2, 3)
    (correction,) = run(
        correction_kernel,
        position,
        (low_3, own_3, high_3, low_d, feed, kill, high_d),
        1,
        3,
        worker=(3,),
    )
    (result,) = run(
        last_kernel, position, (*fourth, correction, ends_c, back), 1, pinned=False, worker=(3,)
    )
    return result[None]


def solution(mesh):
    placed = (P("tm", None, "space", None, None), P("space", None, None), P("space", None, None))
    return jax.shard_map(
        shards,
        mesh=mesh,
        in_specs=placed,
        out_specs=P("tm", None, "space", None, None),
        check_vma=False,
    )
```

```python
import jax
import jax.numpy as jnp
from jax import lax
from jax.experimental import pallas as pl
from jax.experimental.pallas import tpu as pltpu
from jax.sharding import PartitionSpec as P

SUBSTEPS = 4
SWEEPS = 4
FINE_RATES = (0.4, 0.2)
TIME_STEP = 0.25
COARSE_STEP = SUBSTEPS * TIME_STEP
VMEM = pl.BlockSpec(memory_space=pltpu.VMEM)
SMEM = pl.BlockSpec(memory_space=pltpu.SMEM)
ANY = pl.BlockSpec(memory_space=pl.ANY)
AXES = ("tm", "space")


def triple(values, axis):
    pairs = values + pltpu.roll(values, 1, axis)
    return pairs + pltpu.roll(pairs, values.shape[axis] - 1, axis)


def around(values):
    lines = pltpu.roll(values, 1, 0) + pltpu.roll(values, values.shape[0] - 1, 0)
    rows = pltpu.roll(values, 1, 1) + pltpu.roll(values, values.shape[1] - 1, 1)
    return lines + rows


def rates_of(substrate, catalyst, feed, kill):
    encounter = substrate * catalyst * catalyst
    return feed * (1.0 - substrate) - encounter, encounter - (feed + kill) * catalyst


def fine_layer(below, centre, above, feed, kill):
    reactions = rates_of(centre[0], centre[1], feed, kill)
    fields = []
    for species, rate in enumerate(FINE_RATES):
        sums = (below[species] + above[species]) + 2.0 * centre[species]
        sums = triple(triple(sums, 0), 1)
        fields.append(
            (1.0 - 4.0 * rate) * centre[species]
            + (rate / 16.0) * sums
            + TIME_STEP * reactions[species]
        )
    return fields


def sweep_layer(species, below, centre, above, explicit):
    implicit = SUBSTEPS * FINE_RATES[species]
    scale = 1.0 / (1.0 + 6.0 * implicit)
    return scale * explicit + (implicit * scale) * ((below + above) + around(centre))


def explicit_layer(substrate, catalyst, feed, kill):
    first, second = rates_of(substrate, catalyst, feed, kill)
    return substrate + COARSE_STEP * first, catalyst + COARSE_STEP * second


def joined(low, own, high, depth):
    def read(species, layer):
        part = (low, own, high)[layer // depth]
        return part[species, layer % depth]

    return read


def fine_levels(read, coefficient, levels, out, depth):
    count = 3 * depth - 2
    first = levels[0]
    for layer in range(count):
        fields = [[read(species, layer + shift) for species in (0, 1)] for shift in (0, 1, 2)]
        new = fine_layer(*fields, coefficient(0, layer + 1), coefficient(1, layer + 1))
        first[0, layer] = new[0]
        first[1, layer] = new[1]
    source = first
    for substep in range(1, SUBSTEPS):
        count -= 2
        target = out if substep == SUBSTEPS - 1 else levels[substep % 2]
        for layer in range(count):
            place = layer + substep + 1
            fields = [[source[species, layer + shift] for species in (0, 1)] for shift in (0, 1, 2)]
            new = fine_layer(*fields, coefficient(0, place), coefficient(1, place))
            target[0, layer] = new[0]
            target[1, layer] = new[1]
        source = target


def coarse_levels(read, levels, finish, depth):
    count = 3 * depth - 2
    for layer in range(count):
        for species in (0, 1):
            centre = read(species, layer + 1)
            levels[0][species, layer] = sweep_layer(
                species, read(species, layer), centre, read(species, layer + 2), centre
            )
    for sweep in range(1, SWEEPS):
        count -= 2
        source, target = levels[(sweep - 1) % 2], levels[sweep % 2]
        for layer in range(count):
            new = [
                sweep_layer(
                    species,
                    source[species, layer],
                    source[species, layer + 1],
                    source[species, layer + 2],
                    read(species, layer + sweep + 1),
                )
                for species in (0, 1)
            ]
            if sweep == SWEEPS - 1:
                finish(layer, new)
            else:
                target[0, layer] = new[0]
                target[1, layer] = new[1]


def coefficients_of(low, feed, kill, high, depth):
    def coefficient(which, layer):
        if layer < depth:
            return low[which, layer]
        if layer >= 2 * depth:
            return high[which, layer - 2 * depth]
        return (feed, kill)[which][layer - depth]

    return coefficient


def fine_kernel(worker, position, low, own, high, low_c, feed, kill, high_c, explicit, state, *levels):
    depth = own.shape[1]

    @pl.when((position[0] >= worker[0]) & (position[0] <= worker[-1]))
    def _():
        coefficient = coefficients_of(low_c, feed, kill, high_c, depth)
        fine_levels(joined(low, own, high, depth), coefficient, levels, state, depth)
        for layer in range(depth):
            new = explicit_layer(state[0, layer], state[1, layer], feed[layer], kill[layer])
            explicit[0, layer] = new[0]
            explicit[1, layer] = new[1]


def correction_kernel(
    worker, position, low, own, high, low_c, feed, kill, high_c, correction, level_a, level_b, wide
):
    depth = own.shape[1]

    @pl.when((position[0] >= worker[0]) & (position[0] <= worker[-1]))
    def _():
        coefficient = coefficients_of(low_c, feed, kill, high_c, depth)
        read = joined(low, own, high, depth)
        fine_levels(read, coefficient, (level_a, level_b), correction, depth)
        for layer in range(3 * depth):
            new = explicit_layer(
                read(0, layer), read(1, layer), coefficient(0, layer), coefficient(1, layer)
            )
            wide[0, layer] = new[0]
            wide[1, layer] = new[1]

        def finish(layer, new):
            for species in (0, 1):
                correction[species, layer] = correction[species, layer] - new[species]

        coarse_levels(lambda species, layer: wide[species, layer], (level_a, level_b), finish, depth)


def coarse_kernel(worker, position, low, own, high, correction, feed, kill, explicit, state, *levels):
    depth = own.shape[1]

    @pl.when((position[0] >= worker[0]) & (position[0] <= worker[-1]))
    def _():
        def finish(layer, new):
            first = new[0] + correction[0, layer]
            second = new[1] + correction[1, layer]
            state[0, layer] = first
            state[1, layer] = second
            explicit[0, layer], explicit[1, layer] = explicit_layer(
                first, second, feed[layer], kill[layer]
            )

        coarse_levels(joined(low, own, high, depth), levels, finish, depth)


def last_kernel(worker, position, low, own, high, correction, third, state, *levels):
    depth = own.shape[1]

    @pl.when(position[0] != worker[0])
    def _():
        state[...] = third[...]

    @pl.when(position[0] == worker[0])
    def _():
        def finish(layer, new):
            for species in (0, 1):
                state[species, layer] = new[species] + correction[species, layer]

        coarse_levels(joined(low, own, high, depth), levels, finish, depth)


def result_kernel(position, first, second, received, result):
    @pl.when(position[0] == 0)
    def _():
        result[...] = first[...]

    @pl.when(position[0] == 1)
    def _():
        result[...] = second[...]

    @pl.when(position[0] > 1)
    def _():
        result[...] = received[...]


def stack_kernel(position, feed, kill, both):
    both[0] = feed[...]
    both[1] = kill[...]


def pick_kernel(flag, array, other, picked):
    @pl.when(flag[0] != 0)
    def _():
        picked[...] = array[...]

    @pl.when(flag[0] == 0)
    def _():
        picked[...] = other[...]


def run(body, position, operands, outputs, scratch=2, pinned=True, worker=None, tokens=()):
    depth, plane = operands[0].shape[-3], operands[0].shape[-2:]
    shape = (2, depth, *plane)
    if pinned:
        out_shape = [pltpu.VMEM(shape, jnp.float32)] * outputs
    else:
        out_shape = [jax.ShapeDtypeStruct(shape, jnp.float32)] * outputs
    layers = (3 * depth - 2, 3 * depth - 4, 3 * depth)[:scratch]
    operands = [pltpu.with_memory_space_constraint(array, pltpu.VMEM) for array in operands]

    count = 1 + len(operands)

    def kernel(*refs):
        refs = refs[:count] + refs[count + len(tokens) :]
        body(*(() if worker is None else (worker,)), *refs)

    return pl.pallas_call(
        kernel,
        out_shape=out_shape,
        in_specs=[SMEM] + [VMEM] * len(operands) + [ANY] * len(tokens),
        out_specs=[VMEM] * outputs,
        scratch_shapes=[pltpu.VMEM((2, count, *plane), jnp.float32) for count in layers],
        compiler_params=pltpu.CompilerParams(vmem_limit_bytes=12 * 2**20),
        cost_estimate=pl.CostEstimate(
            flops=10**10 if scratch else 10**5, bytes_accessed=2**20, transcendentals=0
        ),
    )(position, *operands, *tokens)


def pick(flag, array, other, tokens=()):
    flag = flag.astype(jnp.int32).reshape(1)
    return run(pick_kernel, flag, (array, other), 1, 0, tokens=tokens)[0]


def shards(starts, feed, kill):
    own = starts[0]
    slabs = lax.axis_size("space")
    ring = 4
    index = lax.axis_index("tm")
    position = index.astype(jnp.int32).reshape(1)
    place = lax.axis_index("space") % ring

    def moved(array, target_of):
        pairs = []
        for source in range(4):
            for slab in range(slabs):
                target = target_of(source, slab)
                if target is not None:
                    pairs.append((source * slabs + slab, target[0] * slabs + target[1] % slabs))
        return lax.ppermute(array, AXES, pairs)

    def beside(slab, step):
        return slab // ring * ring + (slab + step) % ring

    def onward(step):
        return lambda source, slab: (source, slab + step if source < 2 else beside(slab, step))

    def halves(source, slab):
        return onward(1 if source % 2 == 0 else -1)(source, slab)

    def far_half(source, slab):
        if source == 2 and slab % ring == 0:
            return source, slab + ring
        if source == 3 and slab % ring == ring - 1:
            return source, slab - ring
        return None

    def far(source, slab):
        if source >= 2 and slab % ring == 0:
            return source, slab + ring
        if source >= 2 and slab % ring == ring - 1:
            return source, slab - ring
        return None

    def route(source, target, shift=0):
        return lambda origin, slab: (target, slab + shift) if origin == source else None

    def spread(array, source, target):
        low = moved(array, route(source, target, 1))
        high = moved(array, route(source, target, -1))
        return low, moved(array, route(source, target)), high

    (both,) = run(stack_kernel, position, (feed, kill), 1, 0)
    half = moved(both, halves)
    low = moved(own, onward(1))
    high = moved(own, onward(-1))
    half_far = moved(half, far_half)
    lowest = (index >= 2) & (place == 0)
    highest = (index >= 2) & (place == ring - 1)
    half = pick((lowest & (index == 2)) | (highest & (index == 3)), half_far, half)
    other = moved(half, lambda source, slab: (source ^ 1, slab))
    explicit, first_end = run(
        fine_kernel, position, (low, own, high, half, feed, kill, other), 2, worker=(0,)
    )
    second = spread(explicit, 0, 1)
    sides_far = moved(pick(place == 0, low, high), far)
    low = pick(lowest, sides_far, low)
    high = pick(highest, sides_far, high)
    even = index % 2 == 0
    low_c = pick(even, half, other)
    high_c = pick(even, other, half)
    (correction,) = run(
        correction_kernel,
        position,
        (low, own, high, low_c, feed, kill, high_c),
        1,
        3,
        worker=(1, 3),
    )
    crossed = moved(correction, lambda source, slab: (source - 2, slab) if source >= 2 else None)
    explicit, second_end = run(
        coarse_kernel, position, (*second, correction, feed, kill), 2, worker=(1,)
    )
    third = spread(explicit, 1, 0)
    explicit, third_end = run(
        coarse_kernel, position, (*third, crossed, feed, kill), 2, worker=(0,)
    )
    fourth = spread(explicit, 0, 1)
    (last_end,) = run(last_kernel, position, (*fourth, crossed, third_end), 1, worker=(1,))
    received = moved(last_end, lambda source, slab: (source + 2, slab) if source < 2 else None)
    (result,) = run(
        result_kernel, position, (first_end, second_end, received), 1, 0, pinned=False
    )
    return result[None]


def solution(mesh):
    placed = (P("tm", None, "space", None, None), P("space", None, None), P("space", None, None))
    return jax.shard_map(
        shards,
        mesh=mesh,
        in_specs=placed,
        out_specs=P("tm", None, "space", None, None),
        check_vma=False,
    )
```

```python
import jax
import jax.numpy as jnp
from jax import lax
from jax.experimental import pallas as pl
from jax.experimental.pallas import tpu as pltpu
from jax.sharding import PartitionSpec as P

SUBSTEPS = 4
SWEEPS = 4
FINE_RATES = (0.4, 0.2)
TIME_STEP = 0.25
COARSE_STEP = SUBSTEPS * TIME_STEP
VMEM = pl.BlockSpec(memory_space=pltpu.VMEM)
SMEM = pl.BlockSpec(memory_space=pltpu.SMEM)
ANY = pl.BlockSpec(memory_space=pl.ANY)
AXES = ("tm", "space")
SETTLE = 3 * 10**10


def triple(values, axis):
    pairs = values + pltpu.roll(values, 1, axis)
    return pairs + pltpu.roll(pairs, values.shape[axis] - 1, axis)


def around(values):
    lines = pltpu.roll(values, 1, 0) + pltpu.roll(values, values.shape[0] - 1, 0)
    rows = pltpu.roll(values, 1, 1) + pltpu.roll(values, values.shape[1] - 1, 1)
    return lines + rows


def rates_of(substrate, catalyst, feed, kill):
    encounter = substrate * catalyst * catalyst
    return feed * (1.0 - substrate) - encounter, encounter - (feed + kill) * catalyst


def fine_layer(below, centre, above, feed, kill):
    reactions = rates_of(centre[0], centre[1], feed, kill)
    fields = []
    for species, rate in enumerate(FINE_RATES):
        sums = (below[species] + above[species]) + 2.0 * centre[species]
        sums = triple(triple(sums, 0), 1)
        fields.append(
            (1.0 - 4.0 * rate) * centre[species]
            + (rate / 16.0) * sums
            + TIME_STEP * reactions[species]
        )
    return fields


def sweep_layer(species, below, centre, above, explicit):
    implicit = SUBSTEPS * FINE_RATES[species]
    scale = 1.0 / (1.0 + 6.0 * implicit)
    return scale * explicit + (implicit * scale) * ((below + above) + around(centre))


def explicit_layer(substrate, catalyst, feed, kill):
    first, second = rates_of(substrate, catalyst, feed, kill)
    return substrate + COARSE_STEP * first, catalyst + COARSE_STEP * second


def joined(low, own, high, depth):
    def read(species, layer):
        part = (low, own, high)[layer // depth]
        return part[species, layer % depth]

    return read


def fine_levels(read, coefficient, levels, out, depth):
    count = 3 * depth - 2
    first = levels[0]
    for layer in range(count):
        fields = [[read(species, layer + shift) for species in (0, 1)] for shift in (0, 1, 2)]
        new = fine_layer(*fields, coefficient(0, layer + 1), coefficient(1, layer + 1))
        first[0, layer] = new[0]
        first[1, layer] = new[1]
    source = first
    for substep in range(1, SUBSTEPS):
        count -= 2
        target = out if substep == SUBSTEPS - 1 else levels[substep % 2]
        for layer in range(count):
            place = layer + substep + 1
            fields = [[source[species, layer + shift] for species in (0, 1)] for shift in (0, 1, 2)]
            new = fine_layer(*fields, coefficient(0, place), coefficient(1, place))
            target[0, layer] = new[0]
            target[1, layer] = new[1]
        source = target


def coarse_levels(read, levels, finish, depth):
    count = 3 * depth - 2
    for layer in range(count):
        for species in (0, 1):
            centre = read(species, layer + 1)
            levels[0][species, layer] = sweep_layer(
                species, read(species, layer), centre, read(species, layer + 2), centre
            )
    for sweep in range(1, SWEEPS):
        count -= 2
        source, target = levels[(sweep - 1) % 2], levels[sweep % 2]
        for layer in range(count):
            new = [
                sweep_layer(
                    species,
                    source[species, layer],
                    source[species, layer + 1],
                    source[species, layer + 2],
                    read(species, layer + sweep + 1),
                )
                for species in (0, 1)
            ]
            if sweep == SWEEPS - 1:
                finish(layer, new)
            else:
                target[0, layer] = new[0]
                target[1, layer] = new[1]


def fine_kernel(worker, position, low, own, high, low_c, own_c, high_c, explicit, state, *levels):
    depth = own.shape[1]

    @pl.when((position[0] >= worker[0]) & (position[0] <= worker[-1]))
    def _():
        coefficient = joined(low_c, own_c, high_c, depth)
        fine_levels(joined(low, own, high, depth), coefficient, levels, state, depth)
        for layer in range(depth):
            new = explicit_layer(state[0, layer], state[1, layer], own_c[0, layer], own_c[1, layer])
            explicit[0, layer] = new[0]
            explicit[1, layer] = new[1]


def correction_kernel(
    worker, position, low, own, high, low_c, own_c, high_c, correction, level_a, level_b, wide
):
    depth = own.shape[1]

    @pl.when((position[0] >= worker[0]) & (position[0] <= worker[-1]))
    def _():
        coefficient = joined(low_c, own_c, high_c, depth)
        read = joined(low, own, high, depth)
        fine_levels(read, coefficient, (level_a, level_b), correction, depth)
        for layer in range(3 * depth):
            new = explicit_layer(
                read(0, layer), read(1, layer), coefficient(0, layer), coefficient(1, layer)
            )
            wide[0, layer] = new[0]
            wide[1, layer] = new[1]

        def finish(layer, new):
            for species in (0, 1):
                correction[species, layer] = correction[species, layer] - new[species]

        coarse_levels(lambda species, layer: wide[species, layer], (level_a, level_b), finish, depth)


def coarse_kernel(worker, position, low, high, own, correction, own_c, explicit, state, *levels):
    depth = own.shape[1]

    @pl.when((position[0] >= worker[0]) & (position[0] <= worker[-1]))
    def _():
        def finish(layer, new):
            first = new[0] + correction[0, layer]
            second = new[1] + correction[1, layer]
            state[0, layer] = first
            state[1, layer] = second
            explicit[0, layer], explicit[1, layer] = explicit_layer(
                first, second, own_c[0, layer], own_c[1, layer]
            )

        coarse_levels(joined(low, own, high, depth), levels, finish, depth)


def last_kernel(chosen, position, low, high, own, correction, third, state, level_a, level_b):
    depth = own.shape[1]

    @pl.when(position[0] != 1)
    def _():
        state[0] = third[chosen]

    @pl.when(position[0] == 1)
    def _():
        read = joined(low, own, high, depth)
        levels = (level_a, level_b)
        count = 3 * depth - 2
        for sweep in range(SWEEPS):
            for layer in range(count):
                if sweep == 0:
                    parts = [read(chosen, layer + shift) for shift in (0, 1, 2)]
                else:
                    source = levels[(sweep - 1) % 2]
                    parts = [source[chosen, layer + shift] for shift in (0, 1, 2)]
                new = sweep_layer(chosen, *parts, read(chosen, layer + sweep + 1))
                if sweep == SWEEPS - 1:
                    state[0, layer] = new + correction[chosen, layer]
                else:
                    levels[sweep % 2][chosen, layer] = new
            count -= 2


def result_kernel(position, first, second, received_a, received_b, result):
    @pl.when(position[0] == 0)
    def _():
        result[...] = first[...]

    @pl.when(position[0] == 1)
    def _():
        result[...] = second[...]

    @pl.when(position[0] > 1)
    def _():
        result[0] = received_a[0]
        result[1] = received_b[0]


def stack_kernel(feed, kill, both, arrived):
    copies = [
        pltpu.make_async_copy(source, both.at[which], arrived.at[which])
        for which, source in enumerate((feed, kill))
    ]
    for copy in copies:
        copy.start()
    for copy in copies:
        copy.wait()


def stacked(feed, kill):
    return pl.pallas_call(
        stack_kernel,
        out_shape=pltpu.VMEM((2, *feed.shape), feed.dtype),
        in_specs=[ANY, ANY],
        out_specs=VMEM,
        scratch_shapes=[pltpu.SemaphoreType.DMA((2,))],
        compiler_params=pltpu.CompilerParams(vmem_limit_bytes=4 * 2**20),
        cost_estimate=pl.CostEstimate(flops=10**5, bytes_accessed=2**20, transcendentals=0),
    )(feed, kill)


def pick_kernel(flag, array, other, picked):
    @pl.when(flag[0] != 0)
    def _():
        picked[...] = array[...]

    @pl.when(flag[0] == 0)
    def _():
        picked[...] = other[...]


def run(body, position, operands, outputs, scratch=2, pinned=True, worker=None, tokens=(), species=2):
    depth, plane = operands[0].shape[-3], operands[0].shape[-2:]
    shape = (species, depth, *plane)
    if pinned:
        out_shape = [pltpu.VMEM(shape, jnp.float32)] * outputs
    else:
        out_shape = [jax.ShapeDtypeStruct(shape, jnp.float32)] * outputs
    layers = (3 * depth - 2, 3 * depth - 4, 3 * depth)[:scratch]
    operands = [pltpu.with_memory_space_constraint(array, pltpu.VMEM) for array in operands]

    count = 1 + len(operands)

    def kernel(*refs):
        refs = refs[:count] + refs[count + len(tokens) :]
        body(*(() if worker is None else (worker,)), *refs)

    return pl.pallas_call(
        kernel,
        out_shape=out_shape,
        in_specs=[SMEM] + [VMEM] * len(operands) + [ANY] * len(tokens),
        out_specs=[VMEM] * outputs,
        scratch_shapes=[pltpu.VMEM((2, count, *plane), jnp.float32) for count in layers],
        compiler_params=pltpu.CompilerParams(vmem_limit_bytes=12 * 2**20),
        cost_estimate=pl.CostEstimate(
            flops=10**10 if scratch else 10**5, bytes_accessed=2**20, transcendentals=0
        ),
    )(position, *operands, *tokens)


def copy_kernel(array, token, copied):
    copied[...] = array[...]


def after(array, token):
    return pl.pallas_call(
        copy_kernel,
        out_shape=pltpu.VMEM(array.shape, array.dtype),
        in_specs=[VMEM, ANY],
        out_specs=VMEM,
        compiler_params=pltpu.CompilerParams(vmem_limit_bytes=4 * 2**20),
        cost_estimate=pl.CostEstimate(flops=10**5, bytes_accessed=2**20, transcendentals=0),
    )(pltpu.with_memory_space_constraint(array, pltpu.VMEM), token)


def settle_kernel(low, high, low_out, high_out):
    pass


def settled(low, high):
    return pl.pallas_call(
        settle_kernel,
        out_shape=[jax.ShapeDtypeStruct(low.shape, low.dtype)] * 2,
        in_specs=[ANY, ANY],
        out_specs=[ANY, ANY],
        input_output_aliases={0: 0, 1: 1},
        cost_estimate=pl.CostEstimate(flops=SETTLE, bytes_accessed=2**20, transcendentals=0),
    )(
        pltpu.with_memory_space_constraint(low, pltpu.VMEM),
        pltpu.with_memory_space_constraint(high, pltpu.VMEM),
    )


def pick(flag, array, other, tokens=()):
    flag = flag.astype(jnp.int32).reshape(1)
    return run(pick_kernel, flag, (array, other), 1, 0, tokens=tokens)[0]


def shards(starts, feed, kill):
    own = starts[0]
    slabs = lax.axis_size("space")
    ring = 4
    index = lax.axis_index("tm")
    position = index.astype(jnp.int32).reshape(1)
    place = lax.axis_index("space") % ring

    def moved(array, target_of):
        pairs = []
        for source in range(4):
            for slab in range(slabs):
                target = target_of(source, slab)
                if target is not None:
                    pairs.append((source * slabs + slab, target[0] * slabs + target[1] % slabs))
        return lax.ppermute(array, AXES, pairs)

    def beside(slab, step):
        return slab // ring * ring + (slab + step) % ring

    def halves(source, slab):
        step = 1 if source % 2 == 0 else -1
        return source, slab + step if source < 2 else beside(slab, step)

    def around_x(step):
        return lambda source, slab: (source, beside(slab, step)) if source >= 2 else None

    def far_half(source, slab):
        if source == 2 and slab % ring == 0:
            return source, slab + ring
        if source == 3 and slab % ring == ring - 1:
            return source, slab - ring
        return None

    def far(source, slab):
        if source >= 2 and slab % ring == 0:
            return source, slab + ring
        if source >= 2 and slab % ring == ring - 1:
            return source, slab - ring
        return None

    def swapped(source, slab):
        return source ^ 1, slab

    def route(source, target, shift=0):
        return lambda origin, slab: (target, slab + shift) if origin == source else None

    def spread(array, source, target):
        low = moved(array, route(source, target, 1))
        high = moved(array, route(source, target, -1))
        return low, high, moved(array, route(source, target))

    both = stacked(feed, kill)
    half = moved(both, halves)
    low_0 = moved(own, route(0, 0, 1))
    high_0 = moved(own, route(0, 0, -1))
    low_x = moved(own, around_x(1))
    high_x = moved(own, around_x(-1))
    other = moved(half, swapped)
    half_far = moved(half, far_half)
    lowest, highest = place == 0, place == ring - 1
    mended = pick((lowest & (index == 2)) | (highest & (index == 3)), half_far, half)
    other_x = moved(mended, lambda source, slab: swapped(source, slab) if source >= 2 else None)
    own_1 = after(own, half)
    low_1 = moved(own_1, route(1, 1, 1))
    high_1 = moved(own_1, route(1, 1, -1))
    outer = pick(lowest, low_x, high_x)
    outer_far = moved(outer, far)
    low_0, high_0 = settled(low_0, high_0)
    explicit, first_end = run(
        fine_kernel,
        position,
        (low_0, own, high_0, half, both, other),
        2,
        worker=(0,),
        tokens=(outer, own_1),
    )
    second = spread(explicit, 0, 1)
    even = index % 2 == 0
    other = pick(index == 1, other, other_x)
    low_c = pick(even, mended, other)
    high_c = pick(even, other, mended)
    low = pick(index == 1, low_1, pick(lowest, outer_far, low_x))
    high = pick(index == 1, high_1, pick(highest, outer_far, high_x))
    (correction,) = run(
        correction_kernel, position, (low, own, high, low_c, both, high_c), 1, 3, worker=(1, 3)
    )
    crossed_2 = moved(correction, route(2, 0))
    explicit, second_end = run(
        coarse_kernel, position, (*second, correction, both), 2, worker=(1,)
    )
    third = spread(explicit, 1, 0)
    crossed_3 = moved(after(correction, third[0]), route(3, 1))
    explicit, third_end = run(
        coarse_kernel, position, (*third, crossed_2, both), 2, worker=(0,)
    )
    fourth = spread(explicit, 0, 1)
    received = []
    for chosen in (0, 1):
        (last_end,) = run(
            last_kernel, position, (*fourth, crossed_3, third_end), 1, worker=chosen, species=1
        )
        received.append(
            moved(last_end, lambda source, slab: (source + 2, slab) if source < 2 else None)
        )
    (result,) = run(
        result_kernel, position, (first_end, second_end, *received), 1, 0, pinned=False
    )
    return result[None]


def solution(mesh):
    placed = (P("tm", None, "space", None, None), P("space", None, None), P("space", None, None))
    return jax.shard_map(
        shards,
        mesh=mesh,
        in_specs=placed,
        out_specs=P("tm", None, "space", None, None),
        check_vma=False,
    )
```

```python
import jax
import jax.numpy as jnp
from jax import lax
from jax.experimental import pallas as pl
from jax.experimental.pallas import tpu as pltpu
from jax.sharding import PartitionSpec as P

SUBSTEPS = 4
SWEEPS = 4
FINE_RATES = (0.4, 0.2)
TIME_STEP = 0.25
COARSE_STEP = SUBSTEPS * TIME_STEP
VMEM = pl.BlockSpec(memory_space=pltpu.VMEM)
SMEM = pl.BlockSpec(memory_space=pltpu.SMEM)
ANY = pl.BlockSpec(memory_space=pl.ANY)
AXES = ("tm", "space")
SETTLE = 10**9


def triple(values, axis):
    pairs = values + pltpu.roll(values, 1, axis)
    return pairs + pltpu.roll(pairs, values.shape[axis] - 1, axis)


def around(values):
    lines = pltpu.roll(values, 1, 0) + pltpu.roll(values, values.shape[0] - 1, 0)
    rows = pltpu.roll(values, 1, 1) + pltpu.roll(values, values.shape[1] - 1, 1)
    return lines + rows


def rates_of(substrate, catalyst, feed, kill):
    encounter = substrate * catalyst * catalyst
    return feed * (1.0 - substrate) - encounter, encounter - (feed + kill) * catalyst


def fine_layer(below, centre, above, feed, kill):
    reactions = rates_of(centre[0], centre[1], feed, kill)
    fields = []
    for species, rate in enumerate(FINE_RATES):
        sums = (below[species] + above[species]) + 2.0 * centre[species]
        sums = triple(triple(sums, 0), 1)
        fields.append(
            (1.0 - 4.0 * rate) * centre[species]
            + (rate / 16.0) * sums
            + TIME_STEP * reactions[species]
        )
    return fields


def sweep_layer(species, below, centre, above, explicit):
    implicit = SUBSTEPS * FINE_RATES[species]
    scale = 1.0 / (1.0 + 6.0 * implicit)
    return scale * explicit + (implicit * scale) * ((below + above) + around(centre))


def explicit_layer(substrate, catalyst, feed, kill):
    first, second = rates_of(substrate, catalyst, feed, kill)
    return substrate + COARSE_STEP * first, catalyst + COARSE_STEP * second


def joined(low, own, high, depth):
    def read(species, layer):
        part = (low, own, high)[layer // depth]
        return part[species, layer % depth]

    return read


def fine_levels(read, coefficient, levels, out, depth):
    count = 3 * depth - 2
    first = levels[0]
    for layer in range(count):
        fields = [[read(species, layer + shift) for species in (0, 1)] for shift in (0, 1, 2)]
        new = fine_layer(*fields, coefficient(0, layer + 1), coefficient(1, layer + 1))
        first[0, layer] = new[0]
        first[1, layer] = new[1]
    source = first
    for substep in range(1, SUBSTEPS):
        count -= 2
        target = out if substep == SUBSTEPS - 1 else levels[substep % 2]
        for layer in range(count):
            place = layer + substep + 1
            fields = [[source[species, layer + shift] for species in (0, 1)] for shift in (0, 1, 2)]
            new = fine_layer(*fields, coefficient(0, place), coefficient(1, place))
            target[0, layer] = new[0]
            target[1, layer] = new[1]
        source = target


def coarse_levels(read, levels, finish, depth):
    count = 3 * depth - 2
    for layer in range(count):
        for species in (0, 1):
            centre = read(species, layer + 1)
            levels[0][species, layer] = sweep_layer(
                species, read(species, layer), centre, read(species, layer + 2), centre
            )
    for sweep in range(1, SWEEPS):
        count -= 2
        source, target = levels[(sweep - 1) % 2], levels[sweep % 2]
        for layer in range(count):
            new = [
                sweep_layer(
                    species,
                    source[species, layer],
                    source[species, layer + 1],
                    source[species, layer + 2],
                    read(species, layer + sweep + 1),
                )
                for species in (0, 1)
            ]
            if sweep == SWEEPS - 1:
                finish(layer, new)
            else:
                target[0, layer] = new[0]
                target[1, layer] = new[1]


def fine_kernel(worker, position, low, own, high, low_c, own_c, high_c, explicit, state, *levels):
    depth = own.shape[1]

    @pl.when((position[0] >= worker[0]) & (position[0] <= worker[-1]))
    def _():
        coefficient = joined(low_c, own_c, high_c, depth)
        fine_levels(joined(low, own, high, depth), coefficient, levels, state, depth)
        for layer in range(depth):
            new = explicit_layer(state[0, layer], state[1, layer], own_c[0, layer], own_c[1, layer])
            explicit[0, layer] = new[0]
            explicit[1, layer] = new[1]


def correction_kernel(
    worker, position, low, own, high, low_c, own_c, high_c, correction, level_a, level_b, wide
):
    depth = own.shape[1]

    @pl.when((position[0] >= worker[0]) & (position[0] <= worker[-1]))
    def _():
        coefficient = joined(low_c, own_c, high_c, depth)
        read = joined(low, own, high, depth)
        fine_levels(read, coefficient, (level_a, level_b), correction, depth)
        for layer in range(3 * depth):
            new = explicit_layer(
                read(0, layer), read(1, layer), coefficient(0, layer), coefficient(1, layer)
            )
            wide[0, layer] = new[0]
            wide[1, layer] = new[1]

        def finish(layer, new):
            for species in (0, 1):
                correction[species, layer] = correction[species, layer] - new[species]

        coarse_levels(lambda species, layer: wide[species, layer], (level_a, level_b), finish, depth)


def coarse_kernel(worker, position, own, low, high, correction, own_c, explicit, state, *levels):
    depth = own.shape[1]

    @pl.when((position[0] >= worker[0]) & (position[0] <= worker[-1]))
    def _():
        def finish(layer, new):
            first = new[0] + correction[0, layer]
            second = new[1] + correction[1, layer]
            state[0, layer] = first
            state[1, layer] = second
            explicit[0, layer], explicit[1, layer] = explicit_layer(
                first, second, own_c[0, layer], own_c[1, layer]
            )

        coarse_levels(joined(low, own, high, depth), levels, finish, depth)


def last_kernel(chosen, position, own, low, high, correction, third, state, level_a, level_b):
    depth = own.shape[1]

    @pl.when(position[0] != 1)
    def _():
        state[0] = third[chosen]

    @pl.when(position[0] == 1)
    def _():
        read = joined(low, own, high, depth)
        levels = (level_a, level_b)
        count = 3 * depth - 2
        for sweep in range(SWEEPS):
            for layer in range(count):
                if sweep == 0:
                    parts = [read(chosen, layer + shift) for shift in (0, 1, 2)]
                else:
                    source = levels[(sweep - 1) % 2]
                    parts = [source[chosen, layer + shift] for shift in (0, 1, 2)]
                new = sweep_layer(chosen, *parts, read(chosen, layer + sweep + 1))
                if sweep == SWEEPS - 1:
                    state[0, layer] = new + correction[chosen, layer]
                else:
                    levels[sweep % 2][chosen, layer] = new
            count -= 2


def result_kernel(position, first, second, received_a, received_b, result):
    @pl.when(position[0] == 0)
    def _():
        result[...] = first[...]

    @pl.when(position[0] == 1)
    def _():
        result[...] = second[...]

    @pl.when(position[0] > 1)
    def _():
        result[0] = received_a[0]
        result[1] = received_b[0]


def stack_kernel(feed, kill, both, arrived):
    copies = [
        pltpu.make_async_copy(source, both.at[which], arrived.at[which])
        for which, source in enumerate((feed, kill))
    ]
    for copy in copies:
        copy.start()
    for copy in copies:
        copy.wait()


def stacked(feed, kill):
    return pl.pallas_call(
        stack_kernel,
        out_shape=pltpu.VMEM((2, *feed.shape), feed.dtype),
        in_specs=[ANY, ANY],
        out_specs=VMEM,
        scratch_shapes=[pltpu.SemaphoreType.DMA((2,))],
        compiler_params=pltpu.CompilerParams(vmem_limit_bytes=4 * 2**20),
        cost_estimate=pl.CostEstimate(flops=10**5, bytes_accessed=2**20, transcendentals=0),
    )(
        pltpu.with_memory_space_constraint(feed, pltpu.HBM),
        pltpu.with_memory_space_constraint(kill, pltpu.HBM),
    )


def pick_kernel(flag, array, other, picked):
    @pl.when(flag[0] != 0)
    def _():
        picked[...] = array[...]

    @pl.when(flag[0] == 0)
    def _():
        picked[...] = other[...]


def run(body, position, operands, outputs, scratch=2, pinned=True, worker=None, tokens=(), species=2):
    depth, plane = operands[0].shape[-3], operands[0].shape[-2:]
    shape = (species, depth, *plane)
    if pinned:
        out_shape = [pltpu.VMEM(shape, jnp.float32)] * outputs
    else:
        out_shape = [jax.ShapeDtypeStruct(shape, jnp.float32)] * outputs
    layers = (3 * depth - 2, 3 * depth - 4, 3 * depth)[:scratch]
    operands = [pltpu.with_memory_space_constraint(array, pltpu.VMEM) for array in operands]

    count = 1 + len(operands)

    def kernel(*refs):
        refs = refs[:count] + refs[count + len(tokens) :]
        body(*(() if worker is None else (worker,)), *refs)

    return pl.pallas_call(
        kernel,
        out_shape=out_shape,
        in_specs=[SMEM] + [VMEM] * len(operands) + [ANY] * len(tokens),
        out_specs=[VMEM] * outputs,
        scratch_shapes=[pltpu.VMEM((2, count, *plane), jnp.float32) for count in layers],
        compiler_params=pltpu.CompilerParams(vmem_limit_bytes=12 * 2**20),
        cost_estimate=pl.CostEstimate(
            flops=10**10 if scratch else 10**5, bytes_accessed=2**20, transcendentals=0
        ),
    )(position, *operands, *tokens)


def copy_kernel(array, token, copied):
    copied[...] = array[...]


def after(array, token):
    return pl.pallas_call(
        copy_kernel,
        out_shape=pltpu.VMEM(array.shape, array.dtype),
        in_specs=[VMEM, ANY],
        out_specs=VMEM,
        compiler_params=pltpu.CompilerParams(vmem_limit_bytes=4 * 2**20),
        cost_estimate=pl.CostEstimate(flops=10**5, bytes_accessed=2**20, transcendentals=0),
    )(pltpu.with_memory_space_constraint(array, pltpu.VMEM), token)


def settle_kernel(*refs):
    pass


def settled(low, high, tokens):
    return pl.pallas_call(
        settle_kernel,
        out_shape=[jax.ShapeDtypeStruct(low.shape, low.dtype)] * 2,
        in_specs=[ANY] * (2 + len(tokens)),
        out_specs=[ANY, ANY],
        input_output_aliases={0: 0, 1: 1},
        cost_estimate=pl.CostEstimate(flops=SETTLE, bytes_accessed=2**20, transcendentals=0),
    )(
        pltpu.with_memory_space_constraint(low, pltpu.VMEM),
        pltpu.with_memory_space_constraint(high, pltpu.VMEM),
        *tokens,
    )


def pick(flag, array, other, tokens=()):
    flag = flag.astype(jnp.int32).reshape(1)
    return run(pick_kernel, flag, (array, other), 1, 0, tokens=tokens)[0]


def shards(starts, feed, kill):
    own = starts[0]
    slabs = lax.axis_size("space")
    ring = 4
    index = lax.axis_index("tm")
    position = index.astype(jnp.int32).reshape(1)
    place = lax.axis_index("space") % ring

    def moved(array, target_of):
        pairs = []
        for source in range(4):
            for slab in range(slabs):
                target = target_of(source, slab)
                if target is not None:
                    pairs.append((source * slabs + slab, target[0] * slabs + target[1] % slabs))
        return lax.ppermute(array, AXES, pairs)

    def beside(slab, step):
        return slab // ring * ring + (slab + step) % ring

    def halves(source, slab):
        step = 1 if source % 2 == 0 else -1
        return source, slab + step if source < 2 else beside(slab, step)

    def onward(step):
        return lambda source, slab: (source, slab + step) if source < 2 else (source ^ 1, slab)

    def around_x(step):
        return lambda source, slab: (source, beside(slab, step)) if source > 1 else (source ^ 1, slab)

    def far_half(source, slab):
        if source == 2 and slab % ring == 0:
            return source, slab + ring
        if source == 3 and slab % ring == ring - 1:
            return source, slab - ring
        return None

    def far(source, slab):
        if source >= 2 and slab % ring == 0:
            return source, slab + ring
        if source >= 2 and slab % ring == ring - 1:
            return source, slab - ring
        return None

    def swapped(source, slab):
        return source ^ 1, slab

    def route(source, target, shift=0):
        return lambda origin, slab: (target, slab + shift) if origin == source else None

    def spread(array, source, target):
        low = moved(array, route(source, target, 1))
        high = moved(array, route(source, target, -1))
        return moved(array, route(source, target)), low, high

    both = stacked(feed, kill)
    half = moved(both, halves)
    low_x = moved(own, around_x(1))
    high_x = moved(own, around_x(-1))
    low = moved(own, onward(1))
    high = moved(own, onward(-1))
    other = moved(half, swapped)
    half_far = moved(half, far_half)
    lowest, highest = place == 0, place == ring - 1
    outer = pick(lowest, low_x, high_x)
    outer_far = moved(outer, far)
    mended = pick((lowest & (index == 2)) | (highest & (index == 3)), half_far, half)
    other_x = moved(mended, lambda source, slab: swapped(source, slab) if source >= 2 else None)
    low, high = settled(low, high, ())
    low, high = settled(low, high, (outer, mended))
    explicit, first_end = run(
        fine_kernel, position, (low, own, high, half, both, other), 2, worker=(0,)
    )
    second = spread(explicit, 0, 1)
    even = index % 2 == 0
    other = pick(index == 1, other, other_x)
    low_c = pick(even, mended, other)
    high_c = pick(even, other, mended)
    low = pick(index == 1, low, pick(lowest, outer_far, low_x))
    high = pick(index == 1, high, pick(highest, outer_far, high_x))
    (correction,) = run(
        correction_kernel, position, (low, own, high, low_c, both, high_c), 1, 3, worker=(1, 3)
    )
    crossed_2 = moved(correction, route(2, 0))
    explicit, second_end = run(
        coarse_kernel, position, (*second, correction, both), 2, worker=(1,)
    )
    third = spread(explicit, 1, 0)
    crossed_3 = moved(after(correction, third[1]), route(3, 1))
    explicit, third_end = run(
        coarse_kernel, position, (*third, crossed_2, both), 2, worker=(0,)
    )
    fourth = spread(explicit, 0, 1)
    received = []
    for chosen in (0, 1):
        (last_end,) = run(
            last_kernel, position, (*fourth, crossed_3, third_end), 1, worker=chosen, species=1
        )
        received.append(
            moved(last_end, lambda source, slab: (source + 2, slab) if source < 2 else None)
        )
    (result,) = run(
        result_kernel, position, (first_end, second_end, *received), 1, 0, pinned=False
    )
    return result[None]


def solution(mesh):
    placed = (P("tm", None, "space", None, None), P("space", None, None), P("space", None, None))
    return jax.shard_map(
        shards,
        mesh=mesh,
        in_specs=placed,
        out_specs=P("tm", None, "space", None, None),
        check_vma=False,
    )
```

```python
import jax
import jax.numpy as jnp
from jax import lax
from jax.experimental import pallas as pl
from jax.experimental.pallas import tpu as pltpu
from jax.sharding import PartitionSpec as P

SUBSTEPS = 4
SWEEPS = 4
FINE_RATES = (0.4, 0.2)
TIME_STEP = 0.25
COARSE_STEP = SUBSTEPS * TIME_STEP
VMEM = pl.BlockSpec(memory_space=pltpu.VMEM)
SMEM = pl.BlockSpec(memory_space=pltpu.SMEM)
ANY = pl.BlockSpec(memory_space=pl.ANY)
AXES = ("tm", "space")
SETTLE = 10**9


def triple(values, axis):
    pairs = values + pltpu.roll(values, 1, axis)
    return pairs + pltpu.roll(pairs, values.shape[axis] - 1, axis)


def around(values):
    lines = pltpu.roll(values, 1, 0) + pltpu.roll(values, values.shape[0] - 1, 0)
    rows = pltpu.roll(values, 1, 1) + pltpu.roll(values, values.shape[1] - 1, 1)
    return lines + rows


def rates_of(substrate, catalyst, feed, kill):
    encounter = substrate * catalyst * catalyst
    return feed * (1.0 - substrate) - encounter, encounter - (feed + kill) * catalyst


def fine_layer(below, centre, above, feed, kill):
    reactions = rates_of(centre[0], centre[1], feed, kill)
    fields = []
    for species, rate in enumerate(FINE_RATES):
        sums = (below[species] + above[species]) + 2.0 * centre[species]
        sums = triple(triple(sums, 0), 1)
        fields.append(
            (1.0 - 4.0 * rate) * centre[species]
            + (rate / 16.0) * sums
            + TIME_STEP * reactions[species]
        )
    return fields


def sweep_layer(species, below, centre, above, explicit):
    implicit = SUBSTEPS * FINE_RATES[species]
    scale = 1.0 / (1.0 + 6.0 * implicit)
    return scale * explicit + (implicit * scale) * ((below + above) + around(centre))


def explicit_layer(substrate, catalyst, feed, kill):
    first, second = rates_of(substrate, catalyst, feed, kill)
    return substrate + COARSE_STEP * first, catalyst + COARSE_STEP * second


def joined(low, own, high, depth):
    def read(species, layer):
        part = (low, own, high)[layer // depth]
        return part[species, layer % depth]

    return read


def fine_levels(read, coefficient, levels, out, depth):
    count = 3 * depth - 2
    first = levels[0]
    for layer in range(count):
        fields = [[read(species, layer + shift) for species in (0, 1)] for shift in (0, 1, 2)]
        new = fine_layer(*fields, coefficient(0, layer + 1), coefficient(1, layer + 1))
        first[0, layer] = new[0]
        first[1, layer] = new[1]
    source = first
    for substep in range(1, SUBSTEPS):
        count -= 2
        target = out if substep == SUBSTEPS - 1 else levels[substep % 2]
        for layer in range(count):
            place = layer + substep + 1
            fields = [[source[species, layer + shift] for species in (0, 1)] for shift in (0, 1, 2)]
            new = fine_layer(*fields, coefficient(0, place), coefficient(1, place))
            target[0, layer] = new[0]
            target[1, layer] = new[1]
        source = target


def coarse_levels(read, levels, finish, depth):
    count = 3 * depth - 2
    for layer in range(count):
        for species in (0, 1):
            centre = read(species, layer + 1)
            levels[0][species, layer] = sweep_layer(
                species, read(species, layer), centre, read(species, layer + 2), centre
            )
    for sweep in range(1, SWEEPS):
        count -= 2
        source, target = levels[(sweep - 1) % 2], levels[sweep % 2]
        for layer in range(count):
            new = [
                sweep_layer(
                    species,
                    source[species, layer],
                    source[species, layer + 1],
                    source[species, layer + 2],
                    read(species, layer + sweep + 1),
                )
                for species in (0, 1)
            ]
            if sweep == SWEEPS - 1:
                finish(layer, new)
            else:
                target[0, layer] = new[0]
                target[1, layer] = new[1]


def fine_kernel(worker, position, low, own, high, low_c, own_c, high_c, explicit, state, *levels):
    depth = own.shape[1]

    @pl.when((position[0] >= worker[0]) & (position[0] <= worker[-1]))
    def _():
        coefficient = joined(low_c, own_c, high_c, depth)
        fine_levels(joined(low, own, high, depth), coefficient, levels, state, depth)
        for layer in range(depth):
            new = explicit_layer(state[0, layer], state[1, layer], own_c[0, layer], own_c[1, layer])
            explicit[0, layer] = new[0]
            explicit[1, layer] = new[1]


def correction_kernel(
    worker, position, low, own, high, low_c, own_c, high_c, correction, level_a, level_b, wide
):
    depth = own.shape[1]

    @pl.when((position[0] >= worker[0]) & (position[0] <= worker[-1]))
    def _():
        coefficient = joined(low_c, own_c, high_c, depth)
        read = joined(low, own, high, depth)
        fine_levels(read, coefficient, (level_a, level_b), correction, depth)
        for layer in range(3 * depth):
            new = explicit_layer(
                read(0, layer), read(1, layer), coefficient(0, layer), coefficient(1, layer)
            )
            wide[0, layer] = new[0]
            wide[1, layer] = new[1]

        def finish(layer, new):
            for species in (0, 1):
                correction[species, layer] = correction[species, layer] - new[species]

        coarse_levels(lambda species, layer: wide[species, layer], (level_a, level_b), finish, depth)


def coarse_kernel(worker, position, own, low, high, correction, own_c, explicit, state, *levels):
    depth = own.shape[1]

    @pl.when((position[0] >= worker[0]) & (position[0] <= worker[-1]))
    def _():
        def finish(layer, new):
            first = new[0] + correction[0, layer]
            second = new[1] + correction[1, layer]
            state[0, layer] = first
            state[1, layer] = second
            explicit[0, layer], explicit[1, layer] = explicit_layer(
                first, second, own_c[0, layer], own_c[1, layer]
            )

        coarse_levels(joined(low, own, high, depth), levels, finish, depth)


def last_kernel(chosen, position, own, low, high, correction, third, state, level_a, level_b):
    depth = own.shape[1]

    @pl.when(position[0] != 1)
    def _():
        state[0] = third[chosen]

    @pl.when(position[0] == 1)
    def _():
        read = joined(low, own, high, depth)
        levels = (level_a, level_b)
        count = 3 * depth - 2
        for sweep in range(SWEEPS):
            for layer in range(count):
                if sweep == 0:
                    parts = [read(chosen, layer + shift) for shift in (0, 1, 2)]
                else:
                    source = levels[(sweep - 1) % 2]
                    parts = [source[chosen, layer + shift] for shift in (0, 1, 2)]
                new = sweep_layer(chosen, *parts, read(chosen, layer + sweep + 1))
                if sweep == SWEEPS - 1:
                    state[0, layer] = new + correction[chosen, layer]
                else:
                    levels[sweep % 2][chosen, layer] = new
            count -= 2


def result_kernel(position, first, second, received_a, received_b, result):
    @pl.when(position[0] == 0)
    def _():
        result[...] = first[...]

    @pl.when(position[0] == 1)
    def _():
        result[...] = second[...]

    @pl.when(position[0] > 1)
    def _():
        result[0] = received_a[0]
        result[1] = received_b[0]


def stack_kernel(feed, kill, both, arrived):
    copies = [
        pltpu.make_async_copy(source, both.at[which], arrived.at[which])
        for which, source in enumerate((feed, kill))
    ]
    for copy in copies:
        copy.start()
    for copy in copies:
        copy.wait()


def stacked(feed, kill):
    return pl.pallas_call(
        stack_kernel,
        out_shape=pltpu.VMEM((2, *feed.shape), feed.dtype),
        in_specs=[ANY, ANY],
        out_specs=VMEM,
        scratch_shapes=[pltpu.SemaphoreType.DMA((2,))],
        compiler_params=pltpu.CompilerParams(vmem_limit_bytes=4 * 2**20),
        cost_estimate=pl.CostEstimate(flops=10**5, bytes_accessed=2**20, transcendentals=0),
    )(
        pltpu.with_memory_space_constraint(feed, pltpu.HBM),
        pltpu.with_memory_space_constraint(kill, pltpu.HBM),
    )


def pick_kernel(flag, array, other, picked):
    @pl.when(flag[0] != 0)
    def _():
        picked[...] = array[...]

    @pl.when(flag[0] == 0)
    def _():
        picked[...] = other[...]


def run(body, position, operands, outputs, scratch=2, pinned=True, worker=None, tokens=(), species=2):
    depth, plane = operands[0].shape[-3], operands[0].shape[-2:]
    shape = (species, depth, *plane)
    if pinned:
        out_shape = [pltpu.VMEM(shape, jnp.float32)] * outputs
    else:
        out_shape = [jax.ShapeDtypeStruct(shape, jnp.float32)] * outputs
    layers = (3 * depth - 2, 3 * depth - 4, 3 * depth)[:scratch]
    operands = [pltpu.with_memory_space_constraint(array, pltpu.VMEM) for array in operands]

    count = 1 + len(operands)

    def kernel(*refs):
        refs = refs[:count] + refs[count + len(tokens) :]
        body(*(() if worker is None else (worker,)), *refs)

    return pl.pallas_call(
        kernel,
        out_shape=out_shape,
        in_specs=[SMEM] + [VMEM] * len(operands) + [ANY] * len(tokens),
        out_specs=[VMEM] * outputs,
        scratch_shapes=[pltpu.VMEM((2, count, *plane), jnp.float32) for count in layers],
        compiler_params=pltpu.CompilerParams(vmem_limit_bytes=10 * 2**20),
        cost_estimate=pl.CostEstimate(
            flops=10**10 if scratch else 10**5, bytes_accessed=2**20, transcendentals=0
        ),
    )(position, *operands, *tokens)


def copy_kernel(array, token, copied):
    copied[...] = array[...]


def after(array, token):
    return pl.pallas_call(
        copy_kernel,
        out_shape=pltpu.VMEM(array.shape, array.dtype),
        in_specs=[VMEM, ANY],
        out_specs=VMEM,
        compiler_params=pltpu.CompilerParams(vmem_limit_bytes=4 * 2**20),
        cost_estimate=pl.CostEstimate(flops=10**5, bytes_accessed=2**20, transcendentals=0),
    )(pltpu.with_memory_space_constraint(array, pltpu.VMEM), token)


def settle_kernel(*refs):
    pass


def settled(low, high, tokens):
    return pl.pallas_call(
        settle_kernel,
        out_shape=[pltpu.VMEM(low.shape, low.dtype)] * 2,
        in_specs=[ANY] * (2 + len(tokens)),
        out_specs=[ANY, ANY],
        input_output_aliases={0: 0, 1: 1},
        compiler_params=pltpu.CompilerParams(vmem_limit_bytes=2**20),
        cost_estimate=pl.CostEstimate(flops=SETTLE, bytes_accessed=2**20, transcendentals=0),
    )(
        pltpu.with_memory_space_constraint(low, pltpu.VMEM),
        pltpu.with_memory_space_constraint(high, pltpu.VMEM),
        *tokens,
    )


def pick(flag, array, other, tokens=()):
    flag = flag.astype(jnp.int32).reshape(1)
    return run(pick_kernel, flag, (array, other), 1, 0, tokens=tokens)[0]


def shards(starts, feed, kill):
    own = starts[0]
    slabs = lax.axis_size("space")
    ring = 4
    index = lax.axis_index("tm")
    position = index.astype(jnp.int32).reshape(1)
    place = lax.axis_index("space") % ring

    def moved(array, target_of):
        pairs = []
        for source in range(4):
            for slab in range(slabs):
                target = target_of(source, slab)
                if target is not None:
                    pairs.append((source * slabs + slab, target[0] * slabs + target[1] % slabs))
        return lax.ppermute(array, AXES, pairs)

    def beside(slab, step):
        return slab // ring * ring + (slab + step) % ring

    def halves(source, slab):
        step = 1 if source % 2 == 0 else -1
        return source, slab + step if source < 2 else beside(slab, step)

    def onward(step):
        return lambda source, slab: (source, slab + step) if source < 2 else (source ^ 1, slab)

    def around_x(step):
        return lambda source, slab: (source, beside(slab, step)) if source > 1 else (source ^ 1, slab)

    def far_half(source, slab):
        if source == 2 and slab % ring == 0:
            return source, slab + ring
        if source == 3 and slab % ring == ring - 1:
            return source, slab - ring
        return None

    def far(source, slab):
        if source >= 2 and slab % ring == 0:
            return source, slab + ring
        if source >= 2 and slab % ring == ring - 1:
            return source, slab - ring
        return None

    def swapped(source, slab):
        return source ^ 1, slab

    def route(source, target, shift=0):
        return lambda origin, slab: (target, slab + shift) if origin == source else None

    def spread(array, source, target):
        low = moved(array, route(source, target, 1))
        high = moved(array, route(source, target, -1))
        return moved(array, route(source, target)), low, high

    both = stacked(feed, kill)
    half = moved(both, halves)
    low_x = moved(own, around_x(1))
    high_x = moved(own, around_x(-1))
    low = moved(own, onward(1))
    high = moved(own, onward(-1))
    other = moved(half, swapped)
    half_far = moved(half, far_half)
    lowest, highest = place == 0, place == ring - 1
    outer = pick(lowest, low_x, high_x)
    outer_far = moved(outer, far)
    mended = pick((lowest & (index == 2)) | (highest & (index == 3)), half_far, half)
    other_x = moved(mended, lambda source, slab: swapped(source, slab) if source >= 2 else None)
    low, high = settled(low, high, ())
    low, high = settled(low, high, (outer, mended))
    explicit, first_end = run(
        fine_kernel, position, (low, own, high, half, both, other), 2, worker=(0,)
    )
    second = spread(explicit, 0, 1)
    even = index % 2 == 0
    other = pick(index == 1, other, other_x)
    low_c = pick(even, mended, other)
    high_c = pick(even, other, mended)
    low = pick(index == 1, low, pick(lowest, outer_far, low_x))
    high = pick(index == 1, high, pick(highest, outer_far, high_x))
    (correction,) = run(
        correction_kernel, position, (low, own, high, low_c, both, high_c), 1, 3, worker=(1, 3)
    )
    crossed_2 = moved(correction, route(2, 0))
    explicit, second_end = run(
        coarse_kernel, position, (*second, correction, both), 2, worker=(1,)
    )
    third = spread(explicit, 1, 0)
    crossed_3 = moved(after(correction, third[1]), route(3, 1))
    explicit, third_end = run(
        coarse_kernel, position, (*third, crossed_2, both), 2, worker=(0,)
    )
    fourth = spread(explicit, 0, 1)
    received = []
    for chosen in (0, 1):
        (last_end,) = run(
            last_kernel, position, (*fourth, crossed_3, third_end), 1, worker=chosen, species=1
        )
        received.append(
            moved(last_end, lambda source, slab: (source + 2, slab) if source < 2 else None)
        )
    (result,) = run(
        result_kernel, position, (first_end, second_end, *received), 1, 0, pinned=False
    )
    return result[None]


def solution(mesh):
    placed = (P("tm", None, "space", None, None), P("space", None, None), P("space", None, None))
    return jax.shard_map(
        shards,
        mesh=mesh,
        in_specs=placed,
        out_specs=P("tm", None, "space", None, None),
        check_vma=False,
    )
```

```python
import jax
import jax.numpy as jnp
from jax import lax
from jax.experimental import pallas as pl
from jax.experimental.pallas import tpu as pltpu
from jax.sharding import PartitionSpec as P

SUBSTEPS = 4
SWEEPS = 4
FINE_RATES = (0.4, 0.2)
TIME_STEP = 0.25
COARSE_STEP = SUBSTEPS * TIME_STEP
VMEM = pl.BlockSpec(memory_space=pltpu.VMEM)
SMEM = pl.BlockSpec(memory_space=pltpu.SMEM)
ANY = pl.BlockSpec(memory_space=pl.ANY)
AXES = ("tm", "space")
SETTLE = 10**9


def triple(values, axis):
    pairs = values + pltpu.roll(values, 1, axis)
    return pairs + pltpu.roll(pairs, values.shape[axis] - 1, axis)


def around(values):
    lines = pltpu.roll(values, 1, 0) + pltpu.roll(values, values.shape[0] - 1, 0)
    rows = pltpu.roll(values, 1, 1) + pltpu.roll(values, values.shape[1] - 1, 1)
    return lines + rows


def rates_of(substrate, catalyst, feed, kill):
    encounter = substrate * catalyst * catalyst
    return feed * (1.0 - substrate) - encounter, encounter - (feed + kill) * catalyst


def fine_layer(below, centre, above, feed, kill):
    reactions = rates_of(centre[0], centre[1], feed, kill)
    fields = []
    for species, rate in enumerate(FINE_RATES):
        sums = (below[species] + above[species]) + 2.0 * centre[species]
        sums = triple(triple(sums, 0), 1)
        fields.append(
            (1.0 - 4.0 * rate) * centre[species]
            + (rate / 16.0) * sums
            + TIME_STEP * reactions[species]
        )
    return fields


def sweep_layer(species, below, centre, above, explicit):
    implicit = SUBSTEPS * FINE_RATES[species]
    scale = 1.0 / (1.0 + 6.0 * implicit)
    return scale * explicit + (implicit * scale) * ((below + above) + around(centre))


def explicit_layer(substrate, catalyst, feed, kill):
    first, second = rates_of(substrate, catalyst, feed, kill)
    return substrate + COARSE_STEP * first, catalyst + COARSE_STEP * second


def joined(low, own, high, depth):
    def read(species, layer):
        part = (low, own, high)[layer // depth]
        return part[species, layer % depth]

    return read


def fine_levels(read, coefficient, levels, out, depth):
    count = 3 * depth - 2
    first = levels[0]
    for layer in range(count):
        fields = [[read(species, layer + shift) for species in (0, 1)] for shift in (0, 1, 2)]
        new = fine_layer(*fields, coefficient(0, layer + 1), coefficient(1, layer + 1))
        first[0, layer] = new[0]
        first[1, layer] = new[1]
    source = first
    for substep in range(1, SUBSTEPS):
        count -= 2
        target = out if substep == SUBSTEPS - 1 else levels[substep % 2]
        for layer in range(count):
            place = layer + substep + 1
            fields = [[source[species, layer + shift] for species in (0, 1)] for shift in (0, 1, 2)]
            new = fine_layer(*fields, coefficient(0, place), coefficient(1, place))
            target[0, layer] = new[0]
            target[1, layer] = new[1]
        source = target


def coarse_levels(read, levels, finish, depth):
    count = 3 * depth - 2
    for layer in range(count):
        for species in (0, 1):
            centre = read(species, layer + 1)
            levels[0][species, layer] = sweep_layer(
                species, read(species, layer), centre, read(species, layer + 2), centre
            )
    for sweep in range(1, SWEEPS):
        count -= 2
        source, target = levels[(sweep - 1) % 2], levels[sweep % 2]
        for layer in range(count):
            new = [
                sweep_layer(
                    species,
                    source[species, layer],
                    source[species, layer + 1],
                    source[species, layer + 2],
                    read(species, layer + sweep + 1),
                )
                for species in (0, 1)
            ]
            if sweep == SWEEPS - 1:
                finish(layer, new)
            else:
                target[0, layer] = new[0]
                target[1, layer] = new[1]


def fine_kernel(worker, position, low, own, high, low_c, own_c, high_c, explicit, state, *levels):
    depth = own.shape[1]

    @pl.when((position[0] >= worker[0]) & (position[0] <= worker[-1]))
    def _():
        coefficient = joined(low_c, own_c, high_c, depth)
        fine_levels(joined(low, own, high, depth), coefficient, levels, state, depth)
        for layer in range(depth):
            new = explicit_layer(state[0, layer], state[1, layer], own_c[0, layer], own_c[1, layer])
            explicit[0, layer] = new[0]
            explicit[1, layer] = new[1]


def correction_kernel(
    worker, position, low, own, high, low_c, own_c, high_c, correction, level_a, level_b, wide
):
    depth = own.shape[1]

    @pl.when((position[0] >= worker[0]) & (position[0] <= worker[-1]))
    def _():
        coefficient = joined(low_c, own_c, high_c, depth)
        read = joined(low, own, high, depth)
        fine_levels(read, coefficient, (level_a, level_b), correction, depth)
        for layer in range(3 * depth):
            new = explicit_layer(
                read(0, layer), read(1, layer), coefficient(0, layer), coefficient(1, layer)
            )
            wide[0, layer] = new[0]
            wide[1, layer] = new[1]

        def finish(layer, new):
            for species in (0, 1):
                correction[species, layer] = correction[species, layer] - new[species]

        coarse_levels(lambda species, layer: wide[species, layer], (level_a, level_b), finish, depth)


def coarse_kernel(worker, position, own, low, high, correction, own_c, explicit, state, *levels):
    depth = own.shape[1]

    @pl.when((position[0] >= worker[0]) & (position[0] <= worker[-1]))
    def _():
        def finish(layer, new):
            first = new[0] + correction[0, layer]
            second = new[1] + correction[1, layer]
            state[0, layer] = first
            state[1, layer] = second
            explicit[0, layer], explicit[1, layer] = explicit_layer(
                first, second, own_c[0, layer], own_c[1, layer]
            )

        coarse_levels(joined(low, own, high, depth), levels, finish, depth)


def last_kernel(chosen, position, own, low, high, correction, third, state, level_a, level_b):
    depth = own.shape[1]

    @pl.when(position[0] != 1)
    def _():
        state[0] = third[chosen]

    @pl.when(position[0] == 1)
    def _():
        read = joined(low, own, high, depth)
        levels = (level_a, level_b)
        count = 3 * depth - 2
        for sweep in range(SWEEPS):
            for layer in range(count):
                if sweep == 0:
                    parts = [read(chosen, layer + shift) for shift in (0, 1, 2)]
                else:
                    source = levels[(sweep - 1) % 2]
                    parts = [source[chosen, layer + shift] for shift in (0, 1, 2)]
                new = sweep_layer(chosen, *parts, read(chosen, layer + sweep + 1))
                if sweep == SWEEPS - 1:
                    state[0, layer] = new + correction[chosen, layer]
                else:
                    levels[sweep % 2][chosen, layer] = new
            count -= 2


def result_kernel(position, first, second, received_a, received_b, result):
    @pl.when(position[0] == 0)
    def _():
        result[...] = first[...]

    @pl.when(position[0] == 1)
    def _():
        result[...] = second[...]

    @pl.when(position[0] > 1)
    def _():
        result[0] = received_a[0]
        result[1] = received_b[0]


def stack_kernel(feed, kill, both, arrived):
    copies = [
        pltpu.make_async_copy(source, both.at[which], arrived.at[which])
        for which, source in enumerate((feed, kill))
    ]
    for copy in copies:
        copy.start()
    for copy in copies:
        copy.wait()


def stacked(feed, kill):
    return pl.pallas_call(
        stack_kernel,
        out_shape=pltpu.VMEM((2, *feed.shape), feed.dtype),
        in_specs=[ANY, ANY],
        out_specs=VMEM,
        scratch_shapes=[pltpu.SemaphoreType.DMA((2,))],
        compiler_params=pltpu.CompilerParams(vmem_limit_bytes=4 * 2**20),
        cost_estimate=pl.CostEstimate(flops=10**5, bytes_accessed=2**20, transcendentals=0),
    )(
        pltpu.with_memory_space_constraint(feed, pltpu.HBM),
        pltpu.with_memory_space_constraint(kill, pltpu.HBM),
    )


def pick_kernel(flag, array, other, picked):
    @pl.when(flag[0] != 0)
    def _():
        picked[...] = array[...]

    @pl.when(flag[0] == 0)
    def _():
        picked[...] = other[...]


def run(body, position, operands, outputs, scratch=2, pinned=True, worker=None, tokens=(), species=2):
    depth, plane = operands[0].shape[-3], operands[0].shape[-2:]
    shape = (species, depth, *plane)
    if pinned:
        out_shape = [pltpu.VMEM(shape, jnp.float32)] * outputs
    else:
        out_shape = [jax.ShapeDtypeStruct(shape, jnp.float32)] * outputs
    layers = (3 * depth - 2, 3 * depth - 4, 3 * depth)[:scratch]
    operands = [pltpu.with_memory_space_constraint(array, pltpu.VMEM) for array in operands]

    count = 1 + len(operands)

    def kernel(*refs):
        refs = refs[:count] + refs[count + len(tokens) :]
        body(*(() if worker is None else (worker,)), *refs)

    return pl.pallas_call(
        kernel,
        out_shape=out_shape,
        in_specs=[SMEM] + [VMEM] * len(operands) + [ANY] * len(tokens),
        out_specs=[VMEM] * outputs,
        scratch_shapes=[pltpu.VMEM((2, count, *plane), jnp.float32) for count in layers],
        compiler_params=pltpu.CompilerParams(vmem_limit_bytes=10 * 2**20),
        cost_estimate=pl.CostEstimate(
            flops=10**10 if scratch else SETTLE if outputs > 1 else 10**5,
            bytes_accessed=2**20,
            transcendentals=0,
        ),
    )(position, *operands, *tokens)


def copy_kernel(array, token, copied):
    copied[...] = array[...]


def after(array, token):
    return pl.pallas_call(
        copy_kernel,
        out_shape=pltpu.VMEM(array.shape, array.dtype),
        in_specs=[VMEM, ANY],
        out_specs=VMEM,
        compiler_params=pltpu.CompilerParams(vmem_limit_bytes=4 * 2**20),
        cost_estimate=pl.CostEstimate(flops=10**5, bytes_accessed=2**20, transcendentals=0),
    )(pltpu.with_memory_space_constraint(array, pltpu.VMEM), token)


def settle_kernel(flag, low, high, low_out, high_out):
    low_out[...] = low[...]
    high_out[...] = high[...]


def settled(low, high):
    flag = jnp.zeros(1, jnp.int32)
    return run(settle_kernel, flag, (low, high), 2, 0)


def pick(flag, array, other, tokens=()):
    flag = flag.astype(jnp.int32).reshape(1)
    return run(pick_kernel, flag, (array, other), 1, 0, tokens=tokens)[0]


def shards(starts, feed, kill):
    own = starts[0]
    slabs = lax.axis_size("space")
    ring = 4
    index = lax.axis_index("tm")
    position = index.astype(jnp.int32).reshape(1)
    place = lax.axis_index("space") % ring

    def moved(array, target_of):
        pairs = []
        for source in range(4):
            for slab in range(slabs):
                target = target_of(source, slab)
                if target is not None:
                    pairs.append((source * slabs + slab, target[0] * slabs + target[1] % slabs))
        return lax.ppermute(array, AXES, pairs)

    def beside(slab, step):
        return slab // ring * ring + (slab + step) % ring

    def halves(source, slab):
        step = 1 if source % 2 == 0 else -1
        return source, slab + step if source < 2 else beside(slab, step)

    def onward(first, step):
        def target_of(source, slab):
            if source == first:
                return source, slab + step
            return (source, beside(slab, step)) if source == first + 2 else None

        return target_of

    def far_half(source, slab):
        if source == 2 and slab % ring == 0:
            return source, slab + ring
        if source == 3 and slab % ring == ring - 1:
            return source, slab - ring
        return None

    def far(position):
        def target_of(source, slab):
            if source == position and slab % ring == 0:
                return source, slab + ring
            if source == position and slab % ring == ring - 1:
                return source, slab - ring
            return None

        return target_of

    def swapped(source, slab):
        return source ^ 1, slab

    def route(source, target, shift=0):
        return lambda origin, slab: (target, slab + shift) if origin == source else None

    def spread(array, source, target):
        low = moved(array, route(source, target, 1))
        high = moved(array, route(source, target, -1))
        return moved(array, route(source, target)), low, high

    both = stacked(feed, kill)
    half = moved(both, halves)
    low = moved(own, onward(0, 1))
    high = moved(own, onward(0, -1))
    other = moved(half, swapped)
    half_far = moved(half, far_half)
    own_b = after(own, half)
    low_b = moved(own_b, onward(1, 1))
    high_b = moved(own_b, onward(1, -1))
    lowest, highest = place == 0, place == ring - 1
    low, high = settled(low, high)
    outer_2 = moved(pick(lowest, low, high), far(2))
    explicit, first_end = run(
        fine_kernel, position, (low, own, high, half, both, other), 2, worker=(0,), tokens=(own_b,)
    )
    second = spread(explicit, 0, 1)
    mended = pick((lowest & (index == 2)) | (highest & (index == 3)), half_far, half)
    other_x = moved(mended, lambda source, slab: swapped(source, slab) if source >= 2 else None)
    outer_3 = moved(pick(lowest, low_b, high_b, (explicit,)), far(3))
    even = index % 2 == 0
    other = pick(index == 1, other, other_x)
    low_c = pick(even, mended, other)
    high_c = pick(even, other, mended)
    low_2 = pick(index == 1, low_b, pick(lowest, outer_2, low))
    high_2 = pick(index == 1, high_b, pick(highest, outer_2, high))
    (correction,) = run(
        correction_kernel, position, (low_2, own, high_2, low_c, both, high_c), 1, 3, worker=(1, 2)
    )
    crossed_2 = moved(correction, route(2, 0))
    low_3 = pick(lowest, outer_3, low_b)
    high_3 = pick(highest, outer_3, high_b)
    (correction_3,) = run(
        correction_kernel, position, (low_3, own, high_3, low_c, both, high_c), 1, 3, worker=(3, 3)
    )
    explicit, second_end = run(
        coarse_kernel, position, (*second, correction, both), 2, worker=(1,)
    )
    third = spread(explicit, 1, 0)
    crossed_3 = moved(after(correction_3, third[1]), route(3, 1))
    explicit, third_end = run(
        coarse_kernel, position, (*third, crossed_2, both), 2, worker=(0,)
    )
    fourth = spread(explicit, 0, 1)
    received = []
    for chosen in (0, 1):
        (last_end,) = run(
            last_kernel, position, (*fourth, crossed_3, third_end), 1, worker=chosen, species=1
        )
        received.append(
            moved(last_end, lambda source, slab: (source + 2, slab) if source < 2 else None)
        )
    (result,) = run(
        result_kernel, position, (first_end, second_end, *received), 1, 0, pinned=False
    )
    return result[None]


def solution(mesh):
    placed = (P("tm", None, "space", None, None), P("space", None, None), P("space", None, None))
    return jax.shard_map(
        shards,
        mesh=mesh,
        in_specs=placed,
        out_specs=P("tm", None, "space", None, None),
        check_vma=False,
    )
```

```python
from math import comb

import jax
import jax.numpy as jnp
from jax import lax
from jax.experimental import pallas as pl
from jax.experimental.pallas import tpu as pltpu
from jax.sharding import PartitionSpec as P

SUBSTEPS = 4
SWEEPS = 4
FINE_RATES = (0.4, 0.2)
TIME_STEP = 0.25
COARSE_STEP = SUBSTEPS * TIME_STEP
VMEM = pl.BlockSpec(memory_space=pltpu.VMEM)
SMEM = pl.BlockSpec(memory_space=pltpu.SMEM)
ANY = pl.BlockSpec(memory_space=pl.ANY)
AXES = ("tm", "space")
SETTLE = 10**9


ROWS = (16, 8)


def turned(row, shift):
    return pltpu.roll(row, shift % row.shape[1], 1)


class Rows:
    def __init__(self, make):
        self.make = make
        self.made = {}

    def __getitem__(self, row):
        if row not in self.made:
            if row == ROWS[0]:
                self.made[row] = pltpu.roll(self[0], ROWS[1] - 1, 0)
            elif row == -1:
                self.made[row] = pltpu.roll(self[ROWS[0] - 1], 1, 0)
            else:
                self.made[row] = self.make(row)
        return self.made[row]


def fine_layer(below, centre, above, constants, target):
    spread = []
    for species, rate in enumerate(FINE_RATES):

        def column(row, species=species):
            value = centre[species][row]
            return (below[species][row] + above[species][row]) + (value + value)

        columns = Rows(column)
        pairs = Rows(lambda row, columns=columns: columns[row] + columns[row + 1])
        spread.append((rate, pairs))
    for row in range(ROWS[0]):
        sums = []
        for rate, pairs in spread:
            value = pairs[row - 1] + pairs[row]
            value = value + turned(value, 1)
            sums.append((rate / 16.0) * (value + turned(value, -1)))
        substrate, catalyst = centre[0][row], centre[1][row]
        encounter = (substrate * catalyst) * (TIME_STEP * catalyst)
        keep_first, fed, keep_second = [part[row] for part in constants]
        target[0][row] = keep_first * substrate + (fed + sums[0]) - encounter
        target[1][row] = keep_second * catalyst + (sums[1] + encounter)


def explicit_rows(substrate, catalyst, feed, kill):
    encounter = substrate * catalyst * catalyst
    first = (1.0 - COARSE_STEP * feed) * substrate + (COARSE_STEP * feed - COARSE_STEP * encounter)
    second = (1.0 - COARSE_STEP * (feed + kill)) * catalyst + COARSE_STEP * encounter
    return first, second


def explicit_layer(state, coefficient, target):
    for row in range(ROWS[0]):
        target[0][row], target[1][row] = explicit_rows(
            state[0][row], state[1][row], coefficient[0][row], coefficient[1][row]
        )


def joined(low, own, high, depth):
    def layer_of(which, layer):
        part = (low, own, high)[layer // depth]
        return part.at[which, layer % depth]

    return layer_of


def fine_levels(layer_of, coefficient, levels, constants, out, depth, rolled):
    count = 3 * depth - 2
    for layer in range(count):
        for row in range(ROWS[0]):
            feed = TIME_STEP * coefficient(0, layer + 1)[row]
            both = feed + TIME_STEP * coefficient(1, layer + 1)[row]
            constants[0, layer, row] = (1.0 - 4.0 * FINE_RATES[0]) - feed
            constants[1, layer, row] = feed
            constants[2, layer, row] = (1.0 - 4.0 * FINE_RATES[1]) - both
    for substep in range(SUBSTEPS):
        target = out if substep == SUBSTEPS - 1 else levels[substep % 2]

        def step(layer, source, target=target, substep=substep):
            fine_layer(
                *[[source(species, layer + shift) for species in (0, 1)] for shift in (0, 1, 2)],
                [constants.at[which, layer + substep] for which in (0, 1, 2)],
                [target.at[species, layer] for species in (0, 1)],
            )

        if substep == 0:
            for layer in range(count):
                step(layer, layer_of)
            continue
        count -= 2
        held = levels[(substep - 1) % 2]
        source = lambda species, layer, held=held: held.at[species, layer]
        if rolled:

            @pl.loop(0, count, step=2)
            def _(layer, step=step, source=source):
                step(layer, source)
                step(layer + 1, source)

        else:
            for layer in range(count):
                step(layer, source)


def sweep_weights(species):
    implicit = SUBSTEPS * FINE_RATES[species]
    scale = 1.0 / (1.0 + 6.0 * implicit)
    factor = implicit * scale
    powers = [scale * factor**power for power in range(SWEEPS)] + [factor**SWEEPS]
    weights = []
    for plane in range(SWEEPS + 1):
        line = [0.0] * (SWEEPS + 1 - plane)
        for power in range(plane, SWEEPS + 1):
            along = power - plane
            for distance in range(along, -1, -2):
                ways = comb(power, plane) * comb(along, (along - distance) // 2)
                line[distance] += powers[power] * ways
        weights.append(line)
    return weights


def coarse_layer(species, layer_of, layer, put):
    weights = sweep_weights(species)
    centre = layer_of(species, layer)
    sides = [
        (layer_of(species, layer - distance), layer_of(species, layer + distance))
        for distance in range(1, SWEEPS + 1)
    ]
    terms = [[None] * ROWS[0] for _ in range(SWEEPS)]
    first = [None] * ROWS[0]
    for row in range(ROWS[0]):
        sums = [centre[row]] + [below[row] + above[row] for below, above in sides]
        first[row] = weights[SWEEPS][0] * sums[0]
        for plane in range(SWEEPS):
            line = weights[plane]
            total = line[0] * sums[0]
            for distance in range(1, len(line)):
                total = total + line[distance] * sums[distance]
            terms[plane][row] = total
    held = Rows(lambda row, made=first: made[row])
    for plane in range(SWEEPS - 1, -1, -1):
        made = []
        for row in range(ROWS[0]):
            value = held[row]
            around = (held[row - 1] + held[row + 1]) + (turned(value, 1) + turned(value, -1))
            made.append(around + terms[plane][row])
        held = Rows(lambda row, made=made: made[row])
    for row in range(ROWS[0]):
        put(row, held[row])


def fine_kernel(
    worker, position, low, own, high, low_c, own_c, high_c, explicit, state, level_a, level_b, constants
):
    depth = own.shape[1]

    @pl.when((position[0] >= worker[0]) & (position[0] <= worker[-1]))
    def _():
        coefficient = joined(low_c, own_c, high_c, depth)
        layer_of = joined(low, own, high, depth)
        fine_levels(layer_of, coefficient, (level_a, level_b), constants, state, depth, False)
        for layer in range(depth):
            explicit_layer(
                [state.at[species, layer] for species in (0, 1)],
                [own_c.at[which, layer] for which in (0, 1)],
                [explicit.at[species, layer] for species in (0, 1)],
            )


def correction_kernel(
    worker,
    position,
    low,
    own,
    high,
    low_c,
    own_c,
    high_c,
    correction,
    level_a,
    level_b,
    constants,
    wide,
):
    depth = own.shape[1]

    @pl.when((position[0] >= worker[0]) & (position[0] <= worker[-1]))
    def _():
        coefficient = joined(low_c, own_c, high_c, depth)
        layer_of = joined(low, own, high, depth)
        fine_levels(layer_of, coefficient, (level_a, level_b), constants, correction, depth, True)
        for layer in range(3 * depth):
            explicit_layer(
                [layer_of(species, layer) for species in (0, 1)],
                [coefficient(which, layer) for which in (0, 1)],
                [wide.at[species, layer] for species in (0, 1)],
            )

        @pl.loop(0, depth, step=2)
        def _(first):
            for layer in (first, first + 1):
                for species in (0, 1):
                    target = correction.at[species, layer]

                    def put(row, value, target=target):
                        target[row] = target[row] - value

                    coarse_layer(
                        species, lambda which, place: wide.at[which, place], layer + depth, put
                    )


def coarse_kernel(worker, position, low, high, own, correction, own_c, explicit, state):
    depth = own.shape[1]

    @pl.when((position[0] >= worker[0]) & (position[0] <= worker[-1]))
    def _():
        layer_of = joined(low, own, high, depth)
        for layer in range(depth):
            for species in (0, 1):
                target, added = state.at[species, layer], correction.at[species, layer]

                def put(row, value, target=target, added=added):
                    target[row] = value + added[row]

                coarse_layer(species, layer_of, layer + depth, put)
            explicit_layer(
                [state.at[species, layer] for species in (0, 1)],
                [own_c.at[which, layer] for which in (0, 1)],
                [explicit.at[species, layer] for species in (0, 1)],
            )


def last_kernel(chosen, position, low, high, own, correction, third, state):
    depth = own.shape[1]

    @pl.when(position[0] != 1)
    def _():
        state[0] = third[chosen]

    @pl.when(position[0] == 1)
    def _():
        layer_of = joined(low, own, high, depth)
        for layer in range(depth):

            def put(row, value, layer=layer):
                state[0, layer, row] = value + correction[chosen, layer, row]

            coarse_layer(chosen, layer_of, layer + depth, put)


def result_kernel(position, first, second, received_a, received_b, result):
    def put(parts):
        for species in (0, 1):
            array, place = parts[species]
            for layer in range(result.shape[1]):
                for row in range(ROWS[0]):
                    result[species, layer, pl.ds(row, ROWS[1], stride=ROWS[0]), :] = array[
                        place, layer, row
                    ]

    @pl.when(position[0] == 0)
    def _():
        put([(first, 0), (first, 1)])

    @pl.when(position[0] == 1)
    def _():
        put([(second, 0), (second, 1)])

    @pl.when(position[0] > 1)
    def _():
        put([(received_a, 0), (received_b, 0)])


def entry_kernel(state, feed, kill, both, own, held_c, held, arrived):
    parts = ((feed, held_c.at[0]), (kill, held_c.at[1]), (state, held))
    copies = [
        pltpu.make_async_copy(source, target, arrived.at[index])
        for index, (source, target) in enumerate(parts)
    ]
    for copy in copies:
        copy.start()

    def put(array, target):
        for species in (0, 1):
            for layer in range(state.shape[1]):
                for row in range(ROWS[0]):
                    rows = pl.ds(row, ROWS[1], stride=ROWS[0])
                    target[species, layer, row] = array[species, layer, rows, :]

    copies[0].wait()
    copies[1].wait()
    put(held_c, both)
    copies[2].wait()
    put(held, own)


def entered(state, feed, kill):
    depth, _, columns = feed.shape
    shape = pltpu.VMEM((2, depth, *ROWS, columns), feed.dtype)
    return pl.pallas_call(
        entry_kernel,
        out_shape=[shape, shape],
        in_specs=[ANY] * 3,
        out_specs=[VMEM] * 2,
        scratch_shapes=[
            pltpu.VMEM(state.shape, state.dtype),
            pltpu.VMEM(state.shape, state.dtype),
            pltpu.SemaphoreType.DMA((3,)),
        ],
        compiler_params=pltpu.CompilerParams(vmem_limit_bytes=4 * 2**20),
        cost_estimate=pl.CostEstimate(flops=10**5, bytes_accessed=2**20, transcendentals=0),
    )(*[pltpu.with_memory_space_constraint(array, pltpu.HBM) for array in (state, feed, kill)])


LEVELS = ("level_a", "level_b")


def pick_kernel(flag, array, other, picked):
    @pl.when(flag[0] != 0)
    def _():
        picked[...] = array[...]

    @pl.when(flag[0] == 0)
    def _():
        picked[...] = other[...]


def run(
    body, position, operands, outputs, scratch=(), worker=None, tokens=(), species=2, result=None, settling=False
):
    depth, plane = operands[0].shape[1], operands[0].shape[2:]
    if result is None:
        out_shape = [pltpu.VMEM((species, depth, *plane), jnp.float32)] * outputs
    else:
        out_shape = [result]
    wide = 3 * depth
    shapes = {"level_a": (2, wide - 2), "level_b": (2, wide - 4), "constants": (3, wide - 2)}
    shapes["wide"] = (2, wide)
    operands = [pltpu.with_memory_space_constraint(array, pltpu.VMEM) for array in operands]

    count = 1 + len(operands)

    def kernel(*refs):
        refs = refs[:count] + refs[count + len(tokens) :]
        body(*(() if worker is None else (worker,)), *refs)

    return pl.pallas_call(
        kernel,
        out_shape=out_shape,
        in_specs=[SMEM] + [VMEM] * len(operands) + [ANY] * len(tokens),
        out_specs=[VMEM] * outputs,
        scratch_shapes=[pltpu.VMEM((*shapes[name], *plane), jnp.float32) for name in scratch],
        compiler_params=pltpu.CompilerParams(vmem_limit_bytes=10 * 2**20),
        cost_estimate=pl.CostEstimate(
            flops=10**10 if worker is not None else SETTLE if settling else 10**5,
            bytes_accessed=2**20,
            transcendentals=0,
        ),
    )(position, *operands, *tokens)


def copy_kernel(array, token, copied):
    copied[...] = array[...]


def after(array, token):
    return pl.pallas_call(
        copy_kernel,
        out_shape=pltpu.VMEM(array.shape, array.dtype),
        in_specs=[VMEM, ANY],
        out_specs=VMEM,
        compiler_params=pltpu.CompilerParams(vmem_limit_bytes=4 * 2**20),
        cost_estimate=pl.CostEstimate(flops=10**5, bytes_accessed=2**20, transcendentals=0),
    )(pltpu.with_memory_space_constraint(array, pltpu.VMEM), token)


def settle_kernel(flag, *refs):
    for source, target in zip(refs[: len(refs) // 2], refs[len(refs) // 2 :]):
        target[...] = source[...]


def settled(*arrays):
    flag = jnp.zeros(1, jnp.int32)
    return run(settle_kernel, flag, arrays, len(arrays), settling=True)


def pick(flag, array, other, tokens=()):
    flag = flag.astype(jnp.int32).reshape(1)
    return run(pick_kernel, flag, (array, other), 1, tokens=tokens)[0]


def shards(starts, feed, kill):
    own = starts[0]
    slabs = lax.axis_size("space")
    ring = 4
    index = lax.axis_index("tm")
    position = index.astype(jnp.int32).reshape(1)
    place = lax.axis_index("space") % ring

    def moved(array, target_of):
        pairs = []
        for source in range(4):
            for slab in range(slabs):
                target = target_of(source, slab)
                if target is not None:
                    pairs.append((source * slabs + slab, target[0] * slabs + target[1] % slabs))
        return lax.ppermute(array, AXES, pairs)

    def beside(slab, step):
        return slab // ring * ring + (slab + step) % ring

    def halves(source, slab):
        step = 1 if source % 2 == 0 else -1
        return source, slab + step if source < 2 else beside(slab, step)

    def onward(first, step):
        def target_of(source, slab):
            if source == first:
                return source, slab + step
            return (source, beside(slab, step)) if source == first + 2 else None

        return target_of

    def far_half(source, slab):
        if source == 2 and slab % ring == 0:
            return source, slab + ring
        if source == 3 and slab % ring == ring - 1:
            return source, slab - ring
        return None

    def far(position):
        def target_of(source, slab):
            if source == position and slab % ring == 0:
                return source, slab + ring
            if source == position and slab % ring == ring - 1:
                return source, slab - ring
            return None

        return target_of

    def swapped(source, slab):
        return source ^ 1, slab

    def route(source, target, shift=0):
        return lambda origin, slab: (target, slab + shift) if origin == source else None

    def spread(array, source, target, filled=False):
        def upper(origin, slab):
            if origin == source:
                return target, slab - 1
            return (origin ^ 1, slab) if filled else None

        low = moved(array, route(source, target, 1))
        high = moved(array, upper)
        return low, high, moved(array, route(source, target))

    both, own = entered(own, feed, kill)
    half = moved(both, halves)
    low = moved(own, onward(0, 1))
    high = moved(own, onward(0, -1))
    other = moved(half, swapped)
    half_far = moved(half, far_half)
    own_b = after(own, half)
    low_b = moved(own_b, onward(1, 1))
    high_b = moved(own_b, onward(1, -1))
    lowest, highest = place == 0, place == ring - 1
    low, high = settled(low, high)
    outer_2 = moved(pick(lowest, low, high), far(2))
    explicit, first_end = run(
        fine_kernel,
        position,
        (low, own, high, half, both, other),
        2,
        (*LEVELS, "constants"),
        worker=(0,),
        tokens=(own_b,),
    )
    second = spread(explicit, 0, 1)
    mended = pick((lowest & (index == 2)) | (highest & (index == 3)), half_far, half)
    other_x = moved(mended, lambda source, slab: swapped(source, slab) if source >= 2 else None)
    outer_3 = moved(pick(lowest, low_b, high_b, (explicit,)), far(3))
    even = index % 2 == 0
    other = pick(index == 1, other, other_x)
    low_c = pick(even, mended, other)
    high_c = pick(even, other, mended)
    low_2 = pick(index == 1, low_b, pick(lowest, outer_2, low))
    high_2 = pick(index == 1, high_b, pick(highest, outer_2, high))
    (correction,) = run(
        correction_kernel,
        position,
        (low_2, own, high_2, low_c, both, high_c),
        1,
        (*LEVELS, "constants", "wide"),
        worker=(1, 2),
    )
    (crossed_2,) = settled(moved(correction, route(2, 0)))
    low_3 = pick(lowest, outer_3, low_b)
    high_3 = pick(highest, outer_3, high_b)
    (correction_3,) = run(
        correction_kernel,
        position,
        (low_3, own, high_3, low_c, both, high_c),
        1,
        (*LEVELS, "constants", "wide"),
        worker=(3, 3),
    )
    explicit, second_end = run(
        coarse_kernel, position, (*second, correction, both), 2, worker=(1,)
    )
    third = spread(explicit, 1, 0)
    crossed_3 = moved(after(correction_3, third[0]), route(3, 1))
    explicit, third_end = run(
        coarse_kernel, position, (*third, crossed_2, both), 2, worker=(0,)
    )
    fourth = spread(explicit, 0, 1, True)
    received = []
    for chosen in (0, 1):
        (last_end,) = run(
            last_kernel, position, (*fourth, crossed_3, third_end), 1, worker=chosen, species=1
        )
        received.append(
            moved(last_end, lambda source, slab: (source ^ 2, slab))
        )
    (result,) = run(
        result_kernel,
        position,
        (first_end, second_end, *received),
        1,
        result=jax.ShapeDtypeStruct(starts.shape[1:], starts.dtype),
    )
    return result[None]


def solution(mesh):
    placed = (P("tm", None, "space", None, None), P("space", None, None), P("space", None, None))
    return jax.shard_map(
        shards,
        mesh=mesh,
        in_specs=placed,
        out_specs=P("tm", None, "space", None, None),
        check_vma=False,
    )
```

```python
from math import comb

import jax
import jax.numpy as jnp
from jax import lax
from jax.experimental import pallas as pl
from jax.experimental.pallas import tpu as pltpu
from jax.sharding import PartitionSpec as P

SUBSTEPS = 4
SWEEPS = 4
FINE_RATES = (0.4, 0.2)
TIME_STEP = 0.25
COARSE_STEP = SUBSTEPS * TIME_STEP
VMEM = pl.BlockSpec(memory_space=pltpu.VMEM)
SMEM = pl.BlockSpec(memory_space=pltpu.SMEM)
ANY = pl.BlockSpec(memory_space=pl.ANY)
AXES = ("tm", "space")
SETTLE = 10**9


ROWS = (16, 8)


def turned(row, shift):
    return pltpu.roll(row, shift % row.shape[1], 1)


class Rows:
    def __init__(self, make):
        self.make = make
        self.made = {}

    def __getitem__(self, row):
        if row not in self.made:
            if row == ROWS[0]:
                self.made[row] = pltpu.roll(self[0], ROWS[1] - 1, 0)
            elif row == -1:
                self.made[row] = pltpu.roll(self[ROWS[0] - 1], 1, 0)
            else:
                self.made[row] = self.make(row)
        return self.made[row]


def fine_layer(below, centre, above, constants, target):
    spread = []
    for species, rate in enumerate(FINE_RATES):

        def column(row, species=species):
            value = centre[species][row]
            return (below[species][row] + above[species][row]) + (value + value)

        columns = Rows(column)
        pairs = Rows(lambda row, columns=columns: columns[row] + columns[row + 1])
        spread.append((rate, pairs))
    for row in range(ROWS[0]):
        sums = []
        for rate, pairs in spread:
            value = pairs[row - 1] + pairs[row]
            value = value + turned(value, 1)
            sums.append((rate / 16.0) * (value + turned(value, -1)))
        substrate, catalyst = centre[0][row], centre[1][row]
        encounter = (substrate * catalyst) * (TIME_STEP * catalyst)
        keep_first, fed, keep_second = [part[row] for part in constants]
        target[0][row] = keep_first * substrate + (fed + sums[0]) - encounter
        target[1][row] = keep_second * catalyst + (sums[1] + encounter)


def explicit_rows(substrate, catalyst, feed, kill):
    encounter = substrate * catalyst * catalyst
    first = (1.0 - COARSE_STEP * feed) * substrate + (COARSE_STEP * feed - COARSE_STEP * encounter)
    second = (1.0 - COARSE_STEP * (feed + kill)) * catalyst + COARSE_STEP * encounter
    return first, second


def explicit_layer(state, coefficient, target):
    for row in range(ROWS[0]):
        target[0][row], target[1][row] = explicit_rows(
            state[0][row], state[1][row], coefficient[0][row], coefficient[1][row]
        )


def joined(low, own, high, depth):
    def layer_of(which, layer):
        part = (low, own, high)[layer // depth]
        return part.at[which, layer % depth]

    return layer_of


def fine_levels(layer_of, coefficient, levels, constants, out, depth, rolled):
    count = 3 * depth - 2
    for layer in range(count):
        for row in range(ROWS[0]):
            feed = TIME_STEP * coefficient(0, layer + 1)[row]
            both = feed + TIME_STEP * coefficient(1, layer + 1)[row]
            constants[0, layer, row] = (1.0 - 4.0 * FINE_RATES[0]) - feed
            constants[1, layer, row] = feed
            constants[2, layer, row] = (1.0 - 4.0 * FINE_RATES[1]) - both
    for substep in range(SUBSTEPS):
        target = out if substep == SUBSTEPS - 1 else levels[substep % 2]

        def step(layer, source, target=target, substep=substep):
            fine_layer(
                *[[source(species, layer + shift) for species in (0, 1)] for shift in (0, 1, 2)],
                [constants.at[which, layer + substep] for which in (0, 1, 2)],
                [target.at[species, layer] for species in (0, 1)],
            )

        if substep == 0:
            for layer in range(count):
                step(layer, layer_of)
            continue
        count -= 2
        held = levels[(substep - 1) % 2]
        source = lambda species, layer, held=held: held.at[species, layer]
        if rolled:

            @pl.loop(0, count, step=2)
            def _(layer, step=step, source=source):
                step(layer, source)
                step(layer + 1, source)

        else:
            for layer in range(count):
                step(layer, source)


def sweep_weights(species):
    implicit = SUBSTEPS * FINE_RATES[species]
    scale = 1.0 / (1.0 + 6.0 * implicit)
    factor = implicit * scale
    powers = [scale * factor**power for power in range(SWEEPS)] + [factor**SWEEPS]
    weights = []
    for plane in range(SWEEPS + 1):
        line = [0.0] * (SWEEPS + 1 - plane)
        for power in range(plane, SWEEPS + 1):
            along = power - plane
            for distance in range(along, -1, -2):
                ways = comb(power, plane) * comb(along, (along - distance) // 2)
                line[distance] += powers[power] * ways
        weights.append(line)
    return weights


def coarse_layer(species, layer_of, layer, put):
    weights = sweep_weights(species)
    centre = layer_of(species, layer)
    sides = [
        (layer_of(species, layer - distance), layer_of(species, layer + distance))
        for distance in range(1, SWEEPS + 1)
    ]
    terms = [[None] * ROWS[0] for _ in range(SWEEPS)]
    first = [None] * ROWS[0]
    for row in range(ROWS[0]):
        sums = [centre[row]] + [below[row] + above[row] for below, above in sides]
        first[row] = weights[SWEEPS][0] * sums[0]
        for plane in range(SWEEPS):
            line = weights[plane]
            total = line[0] * sums[0]
            for distance in range(1, len(line)):
                total = total + line[distance] * sums[distance]
            terms[plane][row] = total
    held = Rows(lambda row, made=first: made[row])
    for plane in range(SWEEPS - 1, -1, -1):
        made = []
        for row in range(ROWS[0]):
            value = held[row]
            around = (held[row - 1] + held[row + 1]) + (turned(value, 1) + turned(value, -1))
            made.append(around + terms[plane][row])
        held = Rows(lambda row, made=made: made[row])
    for row in range(ROWS[0]):
        put(row, held[row])


def fine_kernel(
    worker, position, low, own, high, low_c, own_c, high_c, explicit, state, level_a, level_b, constants
):
    depth = own.shape[1]

    @pl.when((position[0] >= worker[0]) & (position[0] <= worker[-1]))
    def _():
        coefficient = joined(low_c, own_c, high_c, depth)
        layer_of = joined(low, own, high, depth)
        fine_levels(layer_of, coefficient, (level_a, level_b), constants, state, depth, False)
        for layer in range(depth):
            explicit_layer(
                [state.at[species, layer] for species in (0, 1)],
                [own_c.at[which, layer] for which in (0, 1)],
                [explicit.at[species, layer] for species in (0, 1)],
            )


def correction_kernel(
    worker,
    position,
    low,
    own,
    high,
    low_c,
    own_c,
    high_c,
    correction,
    level_a,
    level_b,
    constants,
    wide,
):
    depth = own.shape[1]

    @pl.when((position[0] >= worker[0]) & (position[0] <= worker[-1]))
    def _():
        coefficient = joined(low_c, own_c, high_c, depth)
        layer_of = joined(low, own, high, depth)
        fine_levels(layer_of, coefficient, (level_a, level_b), constants, correction, depth, True)
        for layer in range(3 * depth):
            explicit_layer(
                [layer_of(species, layer) for species in (0, 1)],
                [coefficient(which, layer) for which in (0, 1)],
                [wide.at[species, layer] for species in (0, 1)],
            )

        @pl.loop(0, depth, step=2)
        def _(first):
            for layer in (first, first + 1):
                for species in (0, 1):
                    target = correction.at[species, layer]

                    def put(row, value, target=target):
                        target[row] = target[row] - value

                    coarse_layer(
                        species, lambda which, place: wide.at[which, place], layer + depth, put
                    )


def coarse_kernel(worker, position, own, low, high, correction, own_c, explicit, state):
    depth = own.shape[1]

    @pl.when((position[0] >= worker[0]) & (position[0] <= worker[-1]))
    def _():
        layer_of = joined(low, own, high, depth)
        for layer in range(depth):
            for species in (0, 1):
                target, added = state.at[species, layer], correction.at[species, layer]

                def put(row, value, target=target, added=added):
                    target[row] = value + added[row]

                coarse_layer(species, layer_of, layer + depth, put)
            explicit_layer(
                [state.at[species, layer] for species in (0, 1)],
                [own_c.at[which, layer] for which in (0, 1)],
                [explicit.at[species, layer] for species in (0, 1)],
            )


def last_kernel(chosen, position, own, low, high, correction, state):
    depth = own.shape[1]

    @pl.when(position[0] == 1)
    def _():
        layer_of = joined(low, own, high, depth)
        for layer in range(depth):

            def put(row, value, layer=layer):
                state[0, layer, row] = value + correction[chosen, layer, row]

            coarse_layer(chosen, layer_of, layer + depth, put)


def result_kernel(position, first, second, third, received_a, received_b, result):
    def put(parts):
        for species in (0, 1):
            array, place = parts[species]
            for layer in range(result.shape[1]):
                for row in range(ROWS[0]):
                    result[species, layer, pl.ds(row, ROWS[1], stride=ROWS[0]), :] = array[
                        place, layer, row
                    ]

    @pl.when(position[0] == 0)
    def _():
        put([(first, 0), (first, 1)])

    @pl.when(position[0] == 1)
    def _():
        put([(second, 0), (second, 1)])

    @pl.when(position[0] == 2)
    def _():
        put([(third, 0), (third, 1)])

    @pl.when(position[0] == 3)
    def _():
        put([(received_a, 0), (received_b, 0)])


def entry_kernel(state, feed, kill, both, own, held_c, held, arrived):
    parts = ((feed, held_c.at[0]), (kill, held_c.at[1]), (state, held))
    copies = [
        pltpu.make_async_copy(source, target, arrived.at[index])
        for index, (source, target) in enumerate(parts)
    ]
    for copy in copies:
        copy.start()

    def put(array, target):
        for species in (0, 1):
            for layer in range(state.shape[1]):
                for row in range(ROWS[0]):
                    rows = pl.ds(row, ROWS[1], stride=ROWS[0])
                    target[species, layer, row] = array[species, layer, rows, :]

    copies[0].wait()
    copies[1].wait()
    put(held_c, both)
    copies[2].wait()
    put(held, own)


def entered(state, feed, kill):
    depth, _, columns = feed.shape
    shape = pltpu.VMEM((2, depth, *ROWS, columns), feed.dtype)
    return pl.pallas_call(
        entry_kernel,
        out_shape=[shape, shape],
        in_specs=[ANY] * 3,
        out_specs=[VMEM] * 2,
        scratch_shapes=[
            pltpu.VMEM(state.shape, state.dtype),
            pltpu.VMEM(state.shape, state.dtype),
            pltpu.SemaphoreType.DMA((3,)),
        ],
        compiler_params=pltpu.CompilerParams(vmem_limit_bytes=4 * 2**20),
        cost_estimate=pl.CostEstimate(flops=10**5, bytes_accessed=2**20, transcendentals=0),
    )(*[pltpu.with_memory_space_constraint(array, pltpu.HBM) for array in (state, feed, kill)])


LEVELS = ("level_a", "level_b")


def pick_kernel(flag, array, other, picked):
    @pl.when(flag[0] != 0)
    def _():
        picked[...] = array[...]

    @pl.when(flag[0] == 0)
    def _():
        picked[...] = other[...]


def run(
    body, position, operands, outputs, scratch=(), worker=None, tokens=(), species=2, result=None, settling=False
):
    depth, plane = operands[0].shape[1], operands[0].shape[2:]
    if result is None:
        out_shape = [pltpu.VMEM((species, depth, *plane), jnp.float32)] * outputs
    else:
        out_shape = [result]
    wide = 3 * depth
    shapes = {"level_a": (2, wide - 2), "level_b": (2, wide - 4), "constants": (3, wide - 2)}
    shapes["wide"] = (2, wide)
    operands = [pltpu.with_memory_space_constraint(array, pltpu.VMEM) for array in operands]

    count = 1 + len(operands)

    def kernel(*refs):
        refs = refs[:count] + refs[count + len(tokens) :]
        body(*(() if worker is None else (worker,)), *refs)

    return pl.pallas_call(
        kernel,
        out_shape=out_shape,
        in_specs=[SMEM] + [VMEM] * len(operands) + [ANY] * len(tokens),
        out_specs=[VMEM] * outputs,
        scratch_shapes=[pltpu.VMEM((*shapes[name], *plane), jnp.float32) for name in scratch],
        compiler_params=pltpu.CompilerParams(vmem_limit_bytes=10 * 2**20),
        cost_estimate=pl.CostEstimate(
            flops=10**10 if worker is not None else SETTLE if settling else 10**5,
            bytes_accessed=2**20,
            transcendentals=0,
        ),
    )(position, *operands, *tokens)


def copy_kernel(array, token, copied):
    copied[...] = array[...]


def after(array, token):
    return pl.pallas_call(
        copy_kernel,
        out_shape=pltpu.VMEM(array.shape, array.dtype),
        in_specs=[VMEM, ANY],
        out_specs=VMEM,
        compiler_params=pltpu.CompilerParams(vmem_limit_bytes=4 * 2**20),
        cost_estimate=pl.CostEstimate(flops=10**5, bytes_accessed=2**20, transcendentals=0),
    )(pltpu.with_memory_space_constraint(array, pltpu.VMEM), token)


def settle_kernel(flag, *refs):
    for source, target in zip(refs[: len(refs) // 2], refs[len(refs) // 2 :]):
        target[...] = source[...]


def settled(*arrays, tokens=()):
    flag = jnp.zeros(1, jnp.int32)
    return run(settle_kernel, flag, arrays, len(arrays), settling=True, tokens=tokens)


def pick(flag, array, other, tokens=()):
    flag = flag.astype(jnp.int32).reshape(1)
    return run(pick_kernel, flag, (array, other), 1, tokens=tokens)[0]


def shards(starts, feed, kill):
    own = starts[0]
    slabs = lax.axis_size("space")
    ring = 4
    index = lax.axis_index("tm")
    position = index.astype(jnp.int32).reshape(1)
    place = lax.axis_index("space") % ring

    def moved(array, target_of):
        pairs = []
        for source in range(4):
            for slab in range(slabs):
                target = target_of(source, slab)
                if target is not None:
                    pairs.append((source * slabs + slab, target[0] * slabs + target[1] % slabs))
        return lax.ppermute(array, AXES, pairs)

    def beside(slab, step):
        return slab // ring * ring + (slab + step) % ring

    def halves(source, slab):
        step = 1 if source % 2 == 0 else -1
        return source, slab + step if source < 2 else beside(slab, step)

    def onward(first, step):
        def target_of(source, slab):
            if source == first:
                return source, slab + step
            return (source, beside(slab, step)) if source == first + 2 else None

        return target_of

    def far_half(source, slab):
        if source == 2 and slab % ring == 0:
            return source, slab + ring
        if source == 3 and slab % ring == ring - 1:
            return source, slab - ring
        return None

    def far(position):
        def target_of(source, slab):
            if source == position and slab % ring == 0:
                return source, slab + ring
            if source == position and slab % ring == ring - 1:
                return source, slab - ring
            return None

        return target_of

    def swapped(source, slab):
        return source ^ 1, slab

    def route(source, target, shift=0):
        return lambda origin, slab: (target, slab + shift) if origin == source else None

    def spread(array, source, target, filled=False):
        def lower(origin, slab):
            if origin == source:
                return target, slab + 1
            return (origin ^ 1, slab) if filled else None

        low = moved(array, lower)
        high = moved(array, route(source, target, -1))
        return moved(array, route(source, target)), low, high

    both, own = entered(own, feed, kill)
    half = moved(both, halves)
    low = moved(own, onward(0, 1))
    high = moved(own, onward(0, -1))
    other = moved(half, swapped)
    half_far = moved(half, far_half)
    own_b = after(own, half)
    low_b = moved(own_b, onward(1, 1))
    high_b = moved(own_b, onward(1, -1))
    lowest, highest = place == 0, place == ring - 1
    (low,) = settled(low)
    outer_2 = moved(pick(lowest, low, high), far(2))
    explicit, first_end = run(
        fine_kernel,
        position,
        (low, own, high, half, both, other),
        2,
        (*LEVELS, "constants"),
        worker=(0,),
        tokens=(own_b,),
    )
    second = spread(explicit, 0, 1)
    mended = pick((lowest & (index == 2)) | (highest & (index == 3)), half_far, half)
    other_x = moved(mended, lambda source, slab: swapped(source, slab) if source >= 2 else None)
    low_b, high_b = settled(low_b, high_b, tokens=(second[0],))
    outer_3 = moved(pick(lowest, low_b, high_b), far(3))
    even = index % 2 == 0
    other = pick(index == 1, other, other_x)
    low_c = pick(even, mended, other)
    high_c = pick(even, other, mended)
    low_2 = pick(index == 1, low_b, pick(lowest, outer_2, low))
    high_2 = pick(index == 1, high_b, pick(highest, outer_2, high))
    (correction,) = run(
        correction_kernel,
        position,
        (low_2, own, high_2, low_c, both, high_c),
        1,
        (*LEVELS, "constants", "wide"),
        worker=(1, 2),
    )
    (crossed_2,) = settled(moved(correction, route(2, 0)))
    low_3 = pick(lowest, outer_3, low_b)
    high_3 = pick(highest, outer_3, high_b)
    (correction_3,) = run(
        correction_kernel,
        position,
        (low_3, own, high_3, low_c, both, high_c),
        1,
        (*LEVELS, "constants", "wide"),
        worker=(3, 3),
    )
    explicit, second_end = run(
        coarse_kernel, position, (*second, correction, both), 2, worker=(1,)
    )
    third = spread(explicit, 1, 0)
    crossed_3 = moved(after(correction_3, third[1]), route(3, 1))
    explicit, third_end = run(
        coarse_kernel, position, (*third, crossed_2, both), 2, worker=(0,)
    )
    fourth = spread(explicit, 0, 1, True)
    third_home = moved(third_end, route(0, 2))
    received = []
    for chosen in (0, 1):
        (last_end,) = run(
            last_kernel,
            position,
            (*fourth, crossed_3),
            1,
            worker=chosen,
            species=1,
            tokens=(third_home,),
        )
        received.append(moved(last_end, lambda source, slab: ((1, 3, 0, 2)[source], slab)))
    (result,) = run(
        result_kernel,
        position,
        (first_end, second_end, third_home, *received),
        1,
        result=jax.ShapeDtypeStruct(starts.shape[1:], starts.dtype),
    )
    return result[None]


def solution(mesh):
    placed = (P("tm", None, "space", None, None), P("space", None, None), P("space", None, None))
    return jax.shard_map(
        shards,
        mesh=mesh,
        in_specs=placed,
        out_specs=P("tm", None, "space", None, None),
        check_vma=False,
    )
```

```python
from math import comb

import jax
import jax.numpy as jnp
from jax import lax
from jax.experimental import pallas as pl
from jax.experimental.pallas import tpu as pltpu
from jax.sharding import PartitionSpec as P

SUBSTEPS = 4
SWEEPS = 4
FINE_RATES = (0.4, 0.2)
TIME_STEP = 0.25
COARSE_STEP = SUBSTEPS * TIME_STEP
VMEM = pl.BlockSpec(memory_space=pltpu.VMEM)
SMEM = pl.BlockSpec(memory_space=pltpu.SMEM)
ANY = pl.BlockSpec(memory_space=pl.ANY)
AXES = ("tm", "space")
SETTLE = 10**9


ROWS = (16, 8)


def turned(row, shift):
    return pltpu.roll(row, shift % row.shape[1], 1)


class Rows:
    def __init__(self, make):
        self.make = make
        self.made = {}

    def __getitem__(self, row):
        if row not in self.made:
            if row == ROWS[0]:
                self.made[row] = pltpu.roll(self[0], ROWS[1] - 1, 0)
            elif row == -1:
                self.made[row] = pltpu.roll(self[ROWS[0] - 1], 1, 0)
            else:
                self.made[row] = self.make(row)
        return self.made[row]


def fine_layer(below, centre, above, constants, target):
    spread = []
    for species, rate in enumerate(FINE_RATES):

        def column(row, species=species):
            value = centre[species][row]
            return (below[species][row] + above[species][row]) + (value + value)

        columns = Rows(column)
        pairs = Rows(lambda row, columns=columns: columns[row] + columns[row + 1])
        spread.append((rate, pairs))
    for row in range(ROWS[0]):
        sums = []
        for rate, pairs in spread:
            value = pairs[row - 1] + pairs[row]
            value = value + turned(value, 1)
            sums.append((rate / 16.0) * (value + turned(value, -1)))
        substrate, catalyst = centre[0][row], centre[1][row]
        encounter = (substrate * catalyst) * (TIME_STEP * catalyst)
        keep_first, fed, keep_second = [part[row] for part in constants]
        target[0][row] = keep_first * substrate + (fed + sums[0]) - encounter
        target[1][row] = keep_second * catalyst + (sums[1] + encounter)


def explicit_rows(substrate, catalyst, feed, kill):
    encounter = substrate * catalyst * catalyst
    first = (1.0 - COARSE_STEP * feed) * substrate + (COARSE_STEP * feed - COARSE_STEP * encounter)
    second = (1.0 - COARSE_STEP * (feed + kill)) * catalyst + COARSE_STEP * encounter
    return first, second


def explicit_layer(state, coefficient, target):
    for row in range(ROWS[0]):
        target[0][row], target[1][row] = explicit_rows(
            state[0][row], state[1][row], coefficient[0][row], coefficient[1][row]
        )


def joined(low, own, high, depth):
    def layer_of(which, layer):
        part = (low, own, high)[layer // depth]
        return part.at[which, layer % depth]

    return layer_of


def fine_levels(layer_of, coefficient, levels, constants, out, depth, rolled):
    count = 3 * depth - 2
    for layer in range(count):
        for row in range(ROWS[0]):
            feed = TIME_STEP * coefficient(0, layer + 1)[row]
            both = feed + TIME_STEP * coefficient(1, layer + 1)[row]
            constants[0, layer, row] = (1.0 - 4.0 * FINE_RATES[0]) - feed
            constants[1, layer, row] = feed
            constants[2, layer, row] = (1.0 - 4.0 * FINE_RATES[1]) - both
    for substep in range(SUBSTEPS):
        target = out if substep == SUBSTEPS - 1 else levels[substep % 2]

        def step(layer, source, target=target, substep=substep):
            fine_layer(
                *[[source(species, layer + shift) for species in (0, 1)] for shift in (0, 1, 2)],
                [constants.at[which, layer + substep] for which in (0, 1, 2)],
                [target.at[species, layer] for species in (0, 1)],
            )

        if substep == 0:
            for layer in range(count):
                step(layer, layer_of)
            continue
        count -= 2
        held = levels[(substep - 1) % 2]
        source = lambda species, layer, held=held: held.at[species, layer]
        if rolled:

            @pl.loop(0, count, step=2)
            def _(layer, step=step, source=source):
                step(layer, source)
                step(layer + 1, source)

        else:
            for layer in range(count):
                step(layer, source)


def sweep_weights(species):
    implicit = SUBSTEPS * FINE_RATES[species]
    scale = 1.0 / (1.0 + 6.0 * implicit)
    factor = implicit * scale
    powers = [scale * factor**power for power in range(SWEEPS)] + [factor**SWEEPS]
    weights = []
    for plane in range(SWEEPS + 1):
        line = [0.0] * (SWEEPS + 1 - plane)
        for power in range(plane, SWEEPS + 1):
            along = power - plane
            for distance in range(along, -1, -2):
                ways = comb(power, plane) * comb(along, (along - distance) // 2)
                line[distance] += powers[power] * ways
        weights.append(line)
    return weights


def coarse_layer(species, layer_of, layer, put):
    weights = sweep_weights(species)
    centre = layer_of(species, layer)
    sides = [
        (layer_of(species, layer - distance), layer_of(species, layer + distance))
        for distance in range(1, SWEEPS + 1)
    ]
    terms = [[None] * ROWS[0] for _ in range(SWEEPS)]
    first = [None] * ROWS[0]
    for row in range(ROWS[0]):
        sums = [centre[row]] + [below[row] + above[row] for below, above in sides]
        first[row] = weights[SWEEPS][0] * sums[0]
        for plane in range(SWEEPS):
            line = weights[plane]
            total = line[0] * sums[0]
            for distance in range(1, len(line)):
                total = total + line[distance] * sums[distance]
            terms[plane][row] = total
    held = Rows(lambda row, made=first: made[row])
    for plane in range(SWEEPS - 1, -1, -1):
        made = []
        for row in range(ROWS[0]):
            value = held[row]
            around = (held[row - 1] + held[row + 1]) + (turned(value, 1) + turned(value, -1))
            made.append(around + terms[plane][row])
        held = Rows(lambda row, made=made: made[row])
    for row in range(ROWS[0]):
        put(row, held[row])


def fine_kernel(
    worker, position, low, own, high, low_c, own_c, high_c, explicit, state, level_a, level_b, constants
):
    depth = own.shape[1]

    @pl.when((position[0] >= worker[0]) & (position[0] <= worker[-1]))
    def _():
        coefficient = joined(low_c, own_c, high_c, depth)
        layer_of = joined(low, own, high, depth)
        fine_levels(layer_of, coefficient, (level_a, level_b), constants, state, depth, False)
        for layer in range(depth):
            explicit_layer(
                [state.at[species, layer] for species in (0, 1)],
                [own_c.at[which, layer] for which in (0, 1)],
                [explicit.at[species, layer] for species in (0, 1)],
            )


def correction_kernel(
    worker,
    position,
    low,
    own,
    high,
    low_c,
    own_c,
    high_c,
    correction,
    level_a,
    level_b,
    constants,
    wide,
):
    depth = own.shape[1]

    @pl.when((position[0] >= worker[0]) & (position[0] <= worker[-1]))
    def _():
        coefficient = joined(low_c, own_c, high_c, depth)
        layer_of = joined(low, own, high, depth)
        fine_levels(layer_of, coefficient, (level_a, level_b), constants, correction, depth, True)
        for layer in range(3 * depth):
            explicit_layer(
                [layer_of(species, layer) for species in (0, 1)],
                [coefficient(which, layer) for which in (0, 1)],
                [wide.at[species, layer] for species in (0, 1)],
            )

        @pl.loop(0, depth, step=2)
        def _(first):
            for layer in (first, first + 1):
                for species in (0, 1):
                    target = correction.at[species, layer]

                    def put(row, value, target=target):
                        target[row] = target[row] - value

                    coarse_layer(
                        species, lambda which, place: wide.at[which, place], layer + depth, put
                    )


def coarse_kernel(worker, position, low, high, own, correction, own_c, explicit, state):
    depth = own.shape[1]

    @pl.when((position[0] >= worker[0]) & (position[0] <= worker[-1]))
    def _():
        layer_of = joined(low, own, high, depth)
        for layer in range(depth):
            for species in (0, 1):
                target, added = state.at[species, layer], correction.at[species, layer]

                def put(row, value, target=target, added=added):
                    target[row] = value + added[row]

                coarse_layer(species, layer_of, layer + depth, put)
            explicit_layer(
                [state.at[species, layer] for species in (0, 1)],
                [own_c.at[which, layer] for which in (0, 1)],
                [explicit.at[species, layer] for species in (0, 1)],
            )


def last_kernel(chosen, position, low, high, own, correction, state):
    depth = own.shape[1]

    @pl.when(position[0] == 1)
    def _():
        layer_of = joined(low, own, high, depth)
        for layer in range(depth):

            def put(row, value, layer=layer):
                state[0, layer, row] = value + correction[chosen, layer, row]

            coarse_layer(chosen, layer_of, layer + depth, put)


def result_kernel(position, first, second, third, received_a, received_b, result):
    def put(parts):
        for species in (0, 1):
            array, place = parts[species]
            for layer in range(result.shape[1]):
                for row in range(ROWS[0]):
                    result[species, layer, pl.ds(row, ROWS[1], stride=ROWS[0]), :] = array[
                        place, layer, row
                    ]

    @pl.when(position[0] == 0)
    def _():
        put([(first, 0), (first, 1)])

    @pl.when(position[0] == 1)
    def _():
        put([(second, 0), (second, 1)])

    @pl.when(position[0] == 2)
    def _():
        put([(third, 0), (third, 1)])

    @pl.when(position[0] == 3)
    def _():
        put([(received_a, 0), (received_b, 0)])


def entry_kernel(state, feed, kill, both, own, held_c, held, arrived):
    parts = ((feed, held_c.at[0]), (kill, held_c.at[1]), (state, held))
    copies = [
        pltpu.make_async_copy(source, target, arrived.at[index])
        for index, (source, target) in enumerate(parts)
    ]
    for copy in copies:
        copy.start()

    def put(array, target):
        for species in (0, 1):
            for layer in range(state.shape[1]):
                for row in range(ROWS[0]):
                    rows = pl.ds(row, ROWS[1], stride=ROWS[0])
                    target[species, layer, row] = array[species, layer, rows, :]

    copies[0].wait()
    copies[1].wait()
    put(held_c, both)
    copies[2].wait()
    put(held, own)


def entered(state, feed, kill):
    depth, _, columns = feed.shape
    shape = pltpu.VMEM((2, depth, *ROWS, columns), feed.dtype)
    return pl.pallas_call(
        entry_kernel,
        out_shape=[shape, shape],
        in_specs=[ANY] * 3,
        out_specs=[VMEM] * 2,
        scratch_shapes=[
            pltpu.VMEM(state.shape, state.dtype),
            pltpu.VMEM(state.shape, state.dtype),
            pltpu.SemaphoreType.DMA((3,)),
        ],
        compiler_params=pltpu.CompilerParams(vmem_limit_bytes=4 * 2**20),
        cost_estimate=pl.CostEstimate(flops=10**5, bytes_accessed=2**20, transcendentals=0),
    )(*[pltpu.with_memory_space_constraint(array, pltpu.HBM) for array in (state, feed, kill)])


LEVELS = ("level_a", "level_b")


def pick_kernel(flag, array, other, picked):
    @pl.when(flag[0] != 0)
    def _():
        picked[...] = array[...]

    @pl.when(flag[0] == 0)
    def _():
        picked[...] = other[...]


def run(
    body, position, operands, outputs, scratch=(), worker=None, tokens=(), species=2, result=None, settling=False
):
    depth, plane = operands[0].shape[1], operands[0].shape[2:]
    if result is None:
        out_shape = [pltpu.VMEM((species, depth, *plane), jnp.float32)] * outputs
    else:
        out_shape = [result]
    wide = 3 * depth
    shapes = {"level_a": (2, wide - 2), "level_b": (2, wide - 4), "constants": (3, wide - 2)}
    shapes["wide"] = (2, wide)
    operands = [pltpu.with_memory_space_constraint(array, pltpu.VMEM) for array in operands]

    count = 1 + len(operands)

    def kernel(*refs):
        refs = refs[:count] + refs[count + len(tokens) :]
        body(*(() if worker is None else (worker,)), *refs)

    return pl.pallas_call(
        kernel,
        out_shape=out_shape,
        in_specs=[SMEM] + [VMEM] * len(operands) + [ANY] * len(tokens),
        out_specs=[VMEM] * outputs,
        scratch_shapes=[pltpu.VMEM((*shapes[name], *plane), jnp.float32) for name in scratch],
        compiler_params=pltpu.CompilerParams(vmem_limit_bytes=10 * 2**20),
        cost_estimate=pl.CostEstimate(
            flops=10**10 if worker is not None else SETTLE if settling else 10**5,
            bytes_accessed=2**20,
            transcendentals=0,
        ),
    )(position, *operands, *tokens)


def copy_kernel(array, token, copied):
    copied[...] = array[...]


def after(array, token):
    return pl.pallas_call(
        copy_kernel,
        out_shape=pltpu.VMEM(array.shape, array.dtype),
        in_specs=[VMEM, ANY],
        out_specs=VMEM,
        compiler_params=pltpu.CompilerParams(vmem_limit_bytes=4 * 2**20),
        cost_estimate=pl.CostEstimate(flops=10**5, bytes_accessed=2**20, transcendentals=0),
    )(pltpu.with_memory_space_constraint(array, pltpu.VMEM), token)


def settle_kernel(flag, *refs):
    for source, target in zip(refs[: len(refs) // 2], refs[len(refs) // 2 :]):
        target[...] = source[...]


def settled(*arrays):
    flag = jnp.zeros(1, jnp.int32)
    return run(settle_kernel, flag, arrays, len(arrays), settling=True)


def pick(flag, array, other, tokens=()):
    flag = flag.astype(jnp.int32).reshape(1)
    return run(pick_kernel, flag, (array, other), 1, tokens=tokens)[0]


def shards(starts, feed, kill):
    own = starts[0]
    slabs = lax.axis_size("space")
    ring = 4
    index = lax.axis_index("tm")
    position = index.astype(jnp.int32).reshape(1)
    place = lax.axis_index("space") % ring

    def moved(array, target_of):
        pairs = []
        for source in range(4):
            for slab in range(slabs):
                target = target_of(source, slab)
                if target is not None:
                    pairs.append((source * slabs + slab, target[0] * slabs + target[1] % slabs))
        return lax.ppermute(array, AXES, pairs)

    def beside(slab, step):
        return slab // ring * ring + (slab + step) % ring

    def halves(source, slab):
        step = 1 if source % 2 == 0 else -1
        return source, slab + step if source < 2 else beside(slab, step)

    def onward(first, step):
        def target_of(source, slab):
            if source == first:
                return source, slab + step
            return (source, beside(slab, step)) if source == first + 2 else None

        return target_of

    def far_half(source, slab):
        if source == 2 and slab % ring == 0:
            return source, slab + ring
        if source == 3 and slab % ring == ring - 1:
            return source, slab - ring
        return None

    def far(position):
        def target_of(source, slab):
            if source == position and slab % ring == 0:
                return source, slab + ring
            if source == position and slab % ring == ring - 1:
                return source, slab - ring
            return None

        return target_of

    def swapped(source, slab):
        return source ^ 1, slab

    def route(source, target, shift=0):
        return lambda origin, slab: (target, slab + shift) if origin == source else None

    def spread(array, source, target, filled=False):
        def upper(origin, slab):
            if origin == source:
                return target, slab - 1
            return (origin ^ 1, slab) if filled else None

        low = moved(array, route(source, target, 1))
        high = moved(array, upper)
        return low, high, moved(array, route(source, target))

    both, own = entered(own, feed, kill)
    half = moved(both, halves)
    low = moved(own, onward(0, 1))
    high = moved(own, onward(0, -1))
    other = moved(half, swapped)
    half_far = moved(half, far_half)
    own_b = after(own, half)
    low_b = moved(own_b, onward(1, 1))
    high_b = moved(own_b, onward(1, -1))
    lowest, highest = place == 0, place == ring - 1
    low, high = settled(low, high)
    outer_2 = moved(pick(lowest, low, high), far(2))
    explicit, first_end = run(
        fine_kernel,
        position,
        (low, own, high, half, both, other),
        2,
        (*LEVELS, "constants"),
        worker=(0,),
        tokens=(own_b,),
    )
    second = spread(explicit, 0, 1)
    mended = pick((lowest & (index == 2)) | (highest & (index == 3)), half_far, half)
    other_x = moved(mended, lambda source, slab: swapped(source, slab) if source >= 2 else None)
    outer_3 = moved(pick(lowest, low_b, high_b, (explicit,)), far(3))
    even = index % 2 == 0
    other = pick(index == 1, other, other_x)
    low_c = pick(even, mended, other)
    high_c = pick(even, other, mended)
    low_2 = pick(index == 1, low_b, pick(lowest, outer_2, low))
    high_2 = pick(index == 1, high_b, pick(highest, outer_2, high))
    (correction,) = run(
        correction_kernel,
        position,
        (low_2, own, high_2, low_c, both, high_c),
        1,
        (*LEVELS, "constants", "wide"),
        worker=(1, 2),
    )
    (crossed_2,) = settled(moved(correction, route(2, 0)))
    low_3 = pick(lowest, outer_3, low_b)
    high_3 = pick(highest, outer_3, high_b)
    (correction_3,) = run(
        correction_kernel,
        position,
        (low_3, own, high_3, low_c, both, high_c),
        1,
        (*LEVELS, "constants", "wide"),
        worker=(3, 3),
    )
    explicit, second_end = run(
        coarse_kernel, position, (*second, correction, both), 2, worker=(1,)
    )
    third = spread(explicit, 1, 0)
    crossed_3 = moved(after(correction_3, third[0]), route(3, 1))
    explicit, third_end = run(
        coarse_kernel, position, (*third, crossed_2, both), 2, worker=(0,)
    )
    fourth = spread(explicit, 0, 1, True)
    third_home = moved(third_end, route(0, 2))
    received = []
    for chosen in (0, 1):
        (last_end,) = run(
            last_kernel,
            position,
            (*fourth, crossed_3),
            1,
            worker=chosen,
            species=1,
            tokens=(third_home,),
        )
        received.append(moved(last_end, lambda source, slab: ((1, 3, 0, 2)[source], slab)))
    (result,) = run(
        result_kernel,
        position,
        (first_end, second_end, third_home, *received),
        1,
        result=jax.ShapeDtypeStruct(starts.shape[1:], starts.dtype),
    )
    return result[None]


def solution(mesh):
    placed = (P("tm", None, "space", None, None), P("space", None, None), P("space", None, None))
    return jax.shard_map(
        shards,
        mesh=mesh,
        in_specs=placed,
        out_specs=P("tm", None, "space", None, None),
        check_vma=False,
    )
```
